32 devices in a mesh: gz: 8 (over y, x, core), gy: 4 (over z).
Axes of the slice: x: 2, y: 2, z: 4, core: 2. Of those that a mesh axis runs over, the one named last changes fastest.
Arguments:
- orbitals: bfloat16 [256, 256, 512], P(('gz', 'gy')), may hold values from -2 to 2
- points: int32 [1024], replicated, may hold values from 0 to 131071, as said below
- coulomb: float32 [256, 512], P(None, 'gy'), may hold values from 10 to 1000
Outputs:
- potentials: bfloat16 [256, 512, 1024], P('gz', 'gy')
The draws below stay inside these ranges and needn't reach their ends.
Inputs may be any that keep to these rules, and one draw needn't show every extreme that they name: `points`: 1024 distinct grid cells.
All inputs are finite; a program needn't handle non-finite values.
Results may differ from the reference program's by a relative error of at most 0.0025.
Values may be sent and summed in bfloat16 or wider, within the bound.
No kernel may reach another device: no remote copies, remote signals or barrier semaphores. Data moves between devices by JAX's collectives and lax.ppermute only.
A program may use at most 192 MiB of HBM per device.

```python
import math
import jax
import jax.numpy as jnp
from jax import lax

BANDS = 256
NPTS = 1024
NZ = 256
COL_DEV = 128
COLS = 512
N_GY = 4


def draw_orbitals(key, part):
    shared_count = 32
    repeats = BANDS // shared_count
    field_key = jax.random.fold_in(key, 11)
    sign_key = jax.random.fold_in(key, 12)
    scale_key = jax.random.fold_in(key, 13)
    noise_key = jax.random.fold_in(key, 14)
    signs = 2.0 * jax.random.bernoulli(sign_key, 0.5, (BANDS,)).astype(jnp.float32) - 1.0
    fields = 0.25 * jax.random.normal(field_key, (shared_count, NZ, COLS), jnp.float32)
    magnitude = jax.random.uniform(scale_key, (BANDS,), jnp.float32, 0.7, 1.3)
    noise = 0.025 * jax.random.normal(noise_key, (BANDS, NZ, COLS), jnp.float32)
    amplitude = (signs * magnitude)[:, None, None]
    shared = jnp.tile(fields, (repeats, 1, 1))
    values = amplitude * shared + noise
    return jnp.clip(values, -2.0, 2.0).astype(jnp.bfloat16)


def draw_points(key, part):
    cell_total = NZ * COLS
    middle_cells = jax.random.permutation(key, cell_total - 2)[:NPTS - 2] + 1
    ends = jnp.array([0, cell_total - 1], dtype=jnp.int32)
    joined = jnp.concatenate([ends, middle_cells.astype(jnp.int32)])
    shuffle = jax.random.permutation(jax.random.fold_in(key, 3), NPTS)
    return jnp.take(joined, shuffle).astype(jnp.int32)


def steps_of(rng, dims, pieces, least, top_value):
    level = 1.0
    for axis_at, blocks in pieces:
        heights = jax.random.uniform(jax.random.fold_in(jax.random.fold_in(rng, 6), axis_at), (blocks,), jnp.float32, least / len(pieces), top_value / len(pieces))
        level = level * jnp.repeat(jnp.exp(heights), dims[axis_at] // blocks).reshape((-1,) + (1,) * (len(dims) - 1 - axis_at))
    return level


def setup_inputs(seed: int = 0) -> dict:
    key_list = jax.random.split(jax.random.key(seed), 4)
    orbitals = draw_orbitals(jax.random.fold_in(key_list[3], 71), 0)
    points = draw_points(jax.random.fold_in(key_list[3], 71), 0)
    coulomb = jnp.clip(jnp.exp(math.log(1000.0) - 4.6051702 * jax.random.uniform(key_list[2], (NZ, COLS), jnp.float32) ** steps_of(key_list[2], (NZ, COLS), ((1, 4),), -0.2, 0.2)), 10.0, 1000.0)
    return dict(orbitals=orbitals, points=points, coulomb=coulomb)


def reference(orbitals, points, coulomb):
    flattened = orbitals.reshape(BANDS, NZ * COLS)
    point_values = jnp.take(flattened, points, axis=1)
    pair_base = lax.dot_general(point_values.astype(jnp.float32), point_values.astype(jnp.float32), (((0,), (0,)), ((), ())), preferred_element_type=jnp.float32)
    pair_gram = pair_base * pair_base
    factor = jnp.linalg.cholesky(pair_gram)
    inverse = jax.scipy.linalg.cho_solve((factor, True), jnp.eye(NPTS, dtype=jnp.float32))

    def one_block(block_index):
        start = (block_index * COL_DEV).astype(jnp.int32)
        column_part = lax.dynamic_slice_in_dim(orbitals, start, COL_DEV, 2)
        kernel_part = lax.dynamic_slice_in_dim(coulomb, start, COL_DEV, 1)
        column_rows = column_part.reshape(BANDS, NZ * COL_DEV)
        sums = lax.dot_general(column_rows.astype(jnp.float32), point_values.astype(jnp.float32), (((0,), (0,)), ((), ())), preferred_element_type=jnp.float32)
        products = sums * sums
        fitted = jnp.dot(products.astype(jnp.float32), inverse.astype(jnp.float32), precision=lax.Precision.HIGHEST, preferred_element_type=jnp.float32)
        fitted = fitted.reshape(NZ, COL_DEV, NPTS)
        spectrum = jnp.fft.fft(fitted, axis=0)
        weighted = spectrum * kernel_part[:, :, None]
        potential = jnp.real(jnp.fft.ifft(weighted, axis=0))
        return potential.astype(jnp.bfloat16)
    blocks = lax.map(one_block, jnp.arange(N_GY, dtype=jnp.int32))
    return jnp.transpose(blocks, (1, 0, 2, 3)).reshape(NZ, COLS, NPTS)
```

```python
import functools
import math

import jax
import jax.numpy as jnp
import numpy as np
from jax import lax
from jax.experimental import pallas as pl
from jax.experimental.pallas import tpu as pltpu
from jax.sharding import PartitionSpec as P

F32 = jnp.float32
BF16 = jnp.bfloat16
HIGH = lax.Precision.HIGHEST
MIB = 1024 * 1024


def split(value):
    high = value.astype(BF16)
    return high, (value - high.astype(F32)).astype(BF16)


def points_kernel(points_ref, field_ref, out_ref, *, columns):
    bands = field_ref.shape[1]
    lane = lax.broadcasted_iota(jnp.int32, (bands, 128), 1)

    def tile(t, _):
        base = pl.multiple_of(t * 128, 128)

        def some(s, acc):
            for u in range(16):
                m = s * 16 + u
                cell = points_ref[base + m]
                plane = cell // columns
                column = cell - plane * columns
                at = pl.multiple_of(plane // 128 * 128, 128)
                row = field_ref[column, :, pl.ds(at, 128)]
                row = pltpu.roll(row, (m - plane + at + 128) % 128, 1)
                acc = jnp.where(lane == m, row, acc)
            return acc

        acc = lax.fori_loop(0, 8, some, jnp.zeros((bands, 128), F32))
        out_ref[:, pl.ds(base, 128)] = acc
        return 0

    lax.fori_loop(0, points_ref.shape[0] // 128, tile, 0)


def take_points(points, field, columns):
    return pl.pallas_call(
        functools.partial(points_kernel, columns=columns),
        out_shape=jax.ShapeDtypeStruct((field.shape[1], points.shape[0]), F32),
        in_specs=[
            pl.BlockSpec(memory_space=pltpu.SMEM),
            pl.BlockSpec(memory_space=pltpu.VMEM),
        ],
        out_specs=pl.BlockSpec(memory_space=pltpu.VMEM),
        compiler_params=pltpu.CompilerParams(vmem_limit_bytes=32 * MIB),
        name="take_points",
    )(points, field)


def sweep_small(a):
    n = a.shape[0]
    lane = lax.broadcasted_iota(jnp.int32, (8, n), 1)
    wide = lax.broadcasted_iota(jnp.int32, (n, n), 1)
    sub = lax.broadcasted_iota(jnp.int32, (8, n), 0)
    for g in range(n // 8):
        lo = 8 * g
        rows = a[lo : lo + 8, :]
        cols = [jnp.broadcast_to(a[:, lo + j : lo + j + 1], (n, n)) for j in range(8)]
        t = [c[lo : lo + 8, :] for c in cols]
        for k in range(8):
            pivot = jnp.broadcast_to(t[k][k : k + 1, :], (8, n))
            scale = 1.0 / pivot
            here = sub == k
            new = []
            for j in range(8):
                if j == k:
                    new.append(jnp.where(here, -scale, t[k] * scale))
                else:
                    factor = jnp.broadcast_to(t[j][k : k + 1, :], (8, n)) * scale
                    new.append(jnp.where(here, factor, t[j] - t[k] * factor))
            t = new
        q = None
        for j in range(8):
            term = t[j] * jnp.broadcast_to(rows[j : j + 1, :], (8, n))
            q = term if q is None else q + term
        q = -q
        for j in range(8):
            q = jnp.where(lane == lo + j, t[j], q)
        inside = (wide >= lo) & (wide < lo + 8)
        upd = jnp.where(inside, 0.0, a)
        for j in range(8):
            upd = upd - cols[j] * jnp.broadcast_to(q[j : j + 1, :], (n, n))
        a = jnp.concatenate(
            ([upd[:lo]] if lo else []) + [q] + ([upd[lo + 8 :]] if lo + 8 < n else []), axis=0
        )
    return a


def mm(a, b):
    return jnp.dot(a, b, precision=HIGH, preferred_element_type=F32)


def inverse_kernel(values_ref, high_ref, low_ref, gram, block, panel, *, big, small):
    n = gram.shape[0]

    @pl.loop(0, n // big)
    def _(t):
        r = pl.ds(pl.multiple_of(t * big, big), big)
        base = lax.dot_general(
            values_ref[:, r], values_ref[...], (((0,), (0,)), ((), ())), preferred_element_type=F32
        )
        gram[r, :] = base * base

    inner = lax.broadcasted_iota(jnp.int32, (small, big), 1)
    inner_full = lax.broadcasted_iota(jnp.int32, (big, big), 1)

    @pl.loop(0, n // big)
    def _(k):
        at = pl.multiple_of(k * big, big)
        kr = pl.ds(at, big)
        block[...] = gram[kr, kr]
        for s in range(big // small):
            lo = s * small
            sr = slice(lo, lo + small)
            negative = sweep_small(block[sr, sr])
            q = -mm(negative, block[sr, :])
            inside = (inner >= lo) & (inner < lo + small)
            q = jnp.where(inside, jnp.concatenate([negative] * (big // small), axis=1), q)
            inside_full = (inner_full >= lo) & (inner_full < lo + small)
            upd = jnp.where(inside_full, 0.0, block[...]) - mm(block[:, sr], q)
            block[...] = upd
            block[sr, :] = q
        panel[...] = -mm(block[...], gram[kr, :])
        panel[:, kr] = block[...]
        wide = lax.broadcasted_iota(jnp.int32, (big, n), 1)
        inside = (wide >= at) & (wide < at + big)

        @pl.loop(0, n // big)
        def _(t):
            r = pl.ds(pl.multiple_of(t * big, big), big)
            col = gram[r, kr]
            gram[r, :] = jnp.where(inside, 0.0, gram[r, :]) - mm(col, panel[...])

        gram[kr, :] = panel[...]

    @pl.loop(0, n // big)
    def _(t):
        r = pl.ds(pl.multiple_of(t * big, big), big)
        high, low = split(-gram[r, :])
        high_ref[r, :] = high
        low_ref[r, :] = low


def invert_gram(values):
    bands, n = values.shape
    big, small = 256, 128
    shape = jax.ShapeDtypeStruct((n, n), BF16)
    return pl.pallas_call(
        functools.partial(inverse_kernel, big=big, small=small),
        out_shape=(shape, shape),
        in_specs=[pl.BlockSpec(memory_space=pltpu.VMEM)],
        out_specs=(pl.BlockSpec(memory_space=pltpu.VMEM),) * 2,
        scratch_shapes=[
            pltpu.VMEM((n, n), F32),
            pltpu.VMEM((big, big), F32),
            pltpu.VMEM((big, n), F32),
        ],
        compiler_params=pltpu.CompilerParams(vmem_limit_bytes=40 * MIB),
        cost_estimate=pl.CostEstimate(
            flops=12 * n**3, bytes_accessed=6 * n * n, transcendentals=0
        ),
        name="invert_gram",
    )(values)


def column_kernel(fields_ref, values_ref, circ_ref, high_ref, low_ref):
    planes_out = high_ref.shape[1]
    for i in range(high_ref.shape[0]):
        field = fields_ref[:, i].reshape(values_ref.shape[0], fields_ref.shape[-1])
        sums = lax.dot_general(
            field, values_ref[...], (((0,), (0,)), ((), ())), preferred_element_type=F32
        )
        high, low = split(sums * sums)
        both = jnp.dot(circ_ref[i], high, preferred_element_type=F32)
        both = both + jnp.dot(circ_ref[i], low, preferred_element_type=F32)
        w_high, w_low = split(both[:planes_out] + both[planes_out:])
        high_ref[i] = w_high
        low_ref[i] = w_low


def convolve(fields, values, circ):
    quads, cols, rows, planes = fields.shape
    bands, n = values.shape
    out_planes = circ.shape[1] // 2
    step = 2
    shape = jax.ShapeDtypeStruct((cols, out_planes, n), BF16)
    out_spec = pl.BlockSpec((step, out_planes, n), lambda j: (j, 0, 0))
    return pl.pallas_call(
        column_kernel,
        grid=(cols // step,),
        out_shape=(shape, shape),
        in_specs=[
            pl.BlockSpec((quads, step, rows, planes), lambda j: (0, j, 0, 0)),
            pl.BlockSpec((bands, n), lambda j: (0, 0)),
            pl.BlockSpec((step, 2 * out_planes, planes), lambda j: (j, 0, 0)),
        ],
        out_specs=(out_spec, out_spec),
        compiler_params=pltpu.CompilerParams(vmem_limit_bytes=40 * MIB),
        cost_estimate=pl.CostEstimate(
            flops=2 * cols * n * planes * (bands + 4 * out_planes),
            bytes_accessed=2 * (quads * cols * rows * planes + 2 * cols * out_planes * n),
            transcendentals=0,
        ),
        name="convolve",
    )(fields, values, circ)


def fit_kernel(w_high_ref, w_low_ref, high_ref, low_ref, out_ref):
    w_high = w_high_ref[...]
    acc = jnp.dot(w_high, high_ref[...], preferred_element_type=F32)
    acc = acc + jnp.dot(w_high, low_ref[...], preferred_element_type=F32)
    acc = acc + jnp.dot(w_low_ref[...], high_ref[...], preferred_element_type=F32)
    out_ref[...] = acc.astype(out_ref.dtype)


def fit(w_high, w_low, high, low):
    rows, n = w_high.shape
    step = 512
    row_spec = pl.BlockSpec((step, n), lambda i: (i, 0))
    full_spec = pl.BlockSpec((n, n), lambda i: (0, 0))
    return pl.pallas_call(
        fit_kernel,
        grid=(rows // step,),
        out_shape=jax.ShapeDtypeStruct((rows, n), BF16),
        in_specs=[row_spec, row_spec, full_spec, full_spec],
        out_specs=row_spec,
        compiler_params=pltpu.CompilerParams(vmem_limit_bytes=48 * MIB),
        cost_estimate=pl.CostEstimate(
            flops=6 * rows * n * n, bytes_accessed=6 * rows * n + 4 * n * n, transcendentals=0
        ),
        name="fit",
    )(w_high, w_low, high, low)


def per_device(orbitals, points, coulomb):
    gz_count = lax.axis_size("gz")
    gy_count = lax.axis_size("gy")
    gz = lax.axis_index("gz")
    gy = lax.axis_index("gy")
    bands_local, planes, columns = orbitals.shape
    col_block = columns // gy_count
    half = col_block // 2
    slab = planes // gz_count
    pairs = gz_count // 2
    me = gz % 2
    pair = gz // 2

    turned = jnp.transpose(orbitals, (2, 0, 1))
    local_values = take_points(points, turned.astype(F32), columns).astype(BF16)
    gathered = lax.all_gather(local_values, ("gz", "gy"), axis=0, tiled=True)

    blocks = turned.reshape(gy_count, 2, half, bands_local, planes)
    slots = []
    for dg in range(gy_count):
        for dc in range(2):
            part = lax.dynamic_slice(
                blocks,
                ((gy + dg) % gy_count, me ^ dc, 0, 0, 0),
                (1, 1, half, bands_local, planes),
            )[0, 0]
            if dg or dc:
                perm = [
                    (z * gy_count + y, (z ^ dc) * gy_count + (y + dg) % gy_count)
                    for z in range(gz_count)
                    for y in range(gy_count)
                ]
                part = lax.ppermute(part, ("gz", "gy"), perm)
            slots.append(part)
    mine = jnp.concatenate(slots, axis=1)
    groups = [[2 * p + c for p in range(pairs)] for c in range(2)]
    fields = lax.all_gather(mine, "gz", axis=0, axis_index_groups=groups)

    slot_ids = jnp.arange(gy_count * 2, dtype=jnp.int32)
    from_gy = (gy - slot_ids // 2) % gy_count
    from_me = me ^ (slot_ids % 2)
    source = (2 * jnp.arange(pairs, dtype=jnp.int32)[:, None] + from_me[None, :]) * gy_count
    source = (source + from_gy[None, :]).reshape(-1)
    ordered = jnp.take(
        gathered.reshape(-1, bands_local, points.shape[0]), source, axis=0
    ).reshape(gathered.shape)

    high, low = invert_gram(gathered)

    grid = np.arange(planes, dtype=np.int64)
    angles = (2.0 * np.pi / planes) * ((grid[:, None] * grid[None, :]) % planes)
    table = np.concatenate([np.cos(angles), np.sin(angles)], axis=1)
    out_rows = lax.dynamic_slice_in_dim(
        jnp.asarray(table, F32), pair * (2 * slab), 2 * slab, 0
    )
    kernel = lax.dynamic_slice_in_dim(coulomb, me * half, half, 1).T
    kernel = jnp.concatenate([kernel, kernel], axis=1)
    weighted = (kernel[:, None, :] * out_rows[None]).reshape(half * 2 * slab, 2 * planes)
    circ = jnp.dot(
        weighted, jnp.asarray(table.T / planes, F32), precision=HIGH, preferred_element_type=F32
    ).reshape(half, 2 * slab, planes)
    coarse = lax.reduce_precision(circ, 8, 7)
    circ = jnp.concatenate([coarse, circ - coarse], axis=1).astype(BF16)

    w_high, w_low = convolve(fields, ordered, circ)
    n = points.shape[0]
    result = fit(w_high.reshape(-1, n), w_low.reshape(-1, n), high, low)
    result = result.reshape(half, 2, slab, n)
    own = lax.dynamic_index_in_dim(result, me, 1, keepdims=False)
    other = lax.dynamic_index_in_dim(result, 1 - me, 1, keepdims=False)
    other = lax.ppermute(other, "gz", [(z, z ^ 1) for z in range(gz_count)])
    first = jnp.where(me == 0, own, other)
    second = jnp.where(me == 0, other, own)
    return jnp.transpose(jnp.concatenate([first, second], axis=0), (1, 0, 2))


def solution(mesh):
    return jax.shard_map(
        per_device,
        mesh=mesh,
        in_specs=(P(("gz", "gy"), None, None), P(), P(None, "gy")),
        out_specs=P("gz", "gy", None),
        check_vma=False,
    )
```

```python
import functools
import math

import jax
import jax.numpy as jnp
import numpy as np
from jax import lax
from jax.experimental import pallas as pl
from jax.experimental.pallas import tpu as pltpu
from jax.sharding import PartitionSpec as P

F32 = jnp.float32
BF16 = jnp.bfloat16
HIGH = lax.Precision.HIGHEST
MIB = 1024 * 1024


def split(value):
    high = value.astype(BF16)
    return high, (value - high.astype(F32)).astype(BF16)


def points_kernel(where_ref, field_ref, out_ref):
    bands = field_ref.shape[1]
    lane = lax.broadcasted_iota(jnp.int32, (bands, 128), 1)

    def tile(t, _):
        base = pl.multiple_of(t * 128, 128)

        def some(s, accs):
            accs = list(accs)
            for u in range(16):
                m = s * 16 + u
                column = where_ref[0, base + m]
                at = pl.multiple_of(where_ref[1, base + m], 128)
                row = field_ref[column, :, pl.ds(at, 128)]
                row = pltpu.roll(row, where_ref[2, base + m], 1)
                accs[u % 4] = jnp.where(lane == m, row, accs[u % 4])
            return tuple(accs)

        accs = lax.fori_loop(0, 8, some, (jnp.zeros((bands, 128), F32),) * 4)
        out_ref[:, pl.ds(base, 128)] = (accs[0] + accs[1]) + (accs[2] + accs[3])
        return 0

    lax.fori_loop(0, out_ref.shape[1] // 128, tile, 0)


def take_points(points, field, columns):
    plane = points // columns
    at = plane // 128 * 128
    shift = (jnp.arange(points.shape[0], dtype=jnp.int32) - plane) % 128
    where = jnp.stack([points - plane * columns, at, shift])
    return pl.pallas_call(
        points_kernel,
        out_shape=jax.ShapeDtypeStruct((field.shape[1], points.shape[0]), F32),
        in_specs=[
            pl.BlockSpec(memory_space=pltpu.SMEM),
            pl.BlockSpec(memory_space=pltpu.VMEM),
        ],
        out_specs=pl.BlockSpec(memory_space=pltpu.VMEM),
        compiler_params=pltpu.CompilerParams(vmem_limit_bytes=32 * MIB),
        name="take_points",
    )(where, field)


def sweep_small(a):
    n = a.shape[0]
    lane = lax.broadcasted_iota(jnp.int32, (8, n), 1)
    wide = lax.broadcasted_iota(jnp.int32, (n, n), 1)
    sub = lax.broadcasted_iota(jnp.int32, (8, n), 0)
    for g in range(n // 8):
        lo = 8 * g
        rows = a[lo : lo + 8, :]
        cols = [jnp.broadcast_to(a[:, lo + j : lo + j + 1], (n, n)) for j in range(8)]
        t = [c[lo : lo + 8, :] for c in cols]
        for k in range(8):
            pivot = jnp.broadcast_to(t[k][k : k + 1, :], (8, n))
            scale = 1.0 / pivot
            here = sub == k
            new = []
            for j in range(8):
                if j == k:
                    new.append(jnp.where(here, -1.0, t[k]) * scale)
                else:
                    factor = jnp.broadcast_to(t[j][k : k + 1, :], (8, n))
                    kept = jnp.where(here, 0.0, t[j])
                    new.append(kept - (jnp.where(here, -1.0, t[k]) * factor) * scale)
            t = new
        terms = [t[j] * jnp.broadcast_to(rows[j : j + 1, :], (8, n)) for j in range(8)]
        while len(terms) > 1:
            terms = [x + y for x, y in zip(terms[::2], terms[1::2])]
        q = -terms[0]
        for j in range(8):
            q = jnp.where(lane == lo + j, t[j], q)
        inside = (wide >= lo) & (wide < lo + 8)
        terms = [cols[j] * jnp.broadcast_to(q[j : j + 1, :], (n, n)) for j in range(8)]
        while len(terms) > 1:
            terms = [x + y for x, y in zip(terms[::2], terms[1::2])]
        upd = jnp.where(inside, 0.0, a) - terms[0]
        a = jnp.concatenate(
            ([upd[:lo]] if lo else []) + [q] + ([upd[lo + 8 :]] if lo + 8 < n else []), axis=0
        )
    return a


def mm(a, b):
    return jnp.dot(a, b, precision=HIGH, preferred_element_type=F32)


def sweep_step(gram, block, panel, k, *, big, small):
    n = gram.shape[0]
    inner = lax.broadcasted_iota(jnp.int32, (small, big), 1)
    inner_full = lax.broadcasted_iota(jnp.int32, (big, big), 1)
    at = k * big
    kr = slice(at, at + big)
    block[...] = gram[kr, kr]
    for s in range(big // small):
        lo = s * small
        sr = slice(lo, lo + small)
        negative = sweep_small(block[sr, sr])
        q = -mm(negative, block[sr, :])
        inside = (inner >= lo) & (inner < lo + small)
        q = jnp.where(inside, jnp.concatenate([negative] * (big // small), axis=1), q)
        inside_full = (inner_full >= lo) & (inner_full < lo + small)
        upd = jnp.where(inside_full, 0.0, block[...]) - mm(block[:, sr], q)
        block[...] = upd
        block[sr, :] = q
    panel[...] = -mm(block[...], gram[kr, :])
    panel[:, kr] = block[...]
    wide = lax.broadcasted_iota(jnp.int32, (big, n), 1)
    inside = (wide >= at) & (wide < at + big)

    @pl.loop(0, n // big)
    def _(t):
        r = pl.ds(pl.multiple_of(t * big, big), big)
        col = gram[r, kr]
        gram[r, :] = jnp.where(inside, 0.0, gram[r, :]) - mm(col, panel[...])

    gram[kr, :] = panel[...]


def first_kernel(values_ref, gram, block, panel, *, big, small):
    @pl.loop(0, gram.shape[0] // big)
    def _(t):
        r = pl.ds(pl.multiple_of(t * big, big), big)
        base = lax.dot_general(
            values_ref[:, r], values_ref[...], (((0,), (0,)), ((), ())), preferred_element_type=F32
        )
        gram[r, :] = base * base

    sweep_step(gram, block, panel, 0, big=big, small=small)


def middle_kernel(*refs, step, big, small):
    gram, block, panel = refs[-3:]
    sweep_step(gram, block, panel, step, big=big, small=small)


def last_kernel(gram_ref, *refs, step, big, small):
    out_ref, gram, block, panel = refs[-4:]
    n = gram.shape[0]
    gram[...] = gram_ref[...]
    sweep_step(gram, block, panel, step, big=big, small=small)

    @pl.loop(0, n // big)
    def _(t):
        at = pl.multiple_of(t * big, big)
        high, low = split(-gram[pl.ds(at, big), :])
        out_ref[pl.ds(at, big), :] = high
        out_ref[pl.ds(at + n, big), :] = low
        out_ref[pl.ds(at + 2 * n, big), :] = high


def sweep_gram(values, gram, step, after):
    big, small = 256, 128
    n = values.shape[1]
    last = step == n // big - 1
    vmem = pl.BlockSpec(memory_space=pltpu.VMEM)
    anywhere = pl.BlockSpec(memory_space=pl.ANY)
    state = jax.ShapeDtypeStruct((n, n), F32)
    scratch = [pltpu.VMEM((big, big), F32), pltpu.VMEM((big, n), F32)]
    options = dict(big=big, small=small)
    params = pltpu.CompilerParams(vmem_limit_bytes=40 * MIB)
    cost = pl.CostEstimate(flops=n**3, bytes_accessed=4 * n * n, transcendentals=0)
    if step == 0:
        return pl.pallas_call(
            functools.partial(first_kernel, **options),
            out_shape=state,
            in_specs=[vmem],
            out_specs=vmem,
            scratch_shapes=scratch,
            compiler_params=params,
            cost_estimate=cost,
            name="sweep_first",
        )(values)
    specs = [vmem] + [anywhere] * len(after)
    if not last:
        return pl.pallas_call(
            functools.partial(middle_kernel, step=step, **options),
            out_shape=state,
            in_specs=specs,
            out_specs=vmem,
            scratch_shapes=scratch,
            input_output_aliases={0: 0},
            compiler_params=params,
            cost_estimate=cost,
            name="sweep_middle",
        )(gram, *after)
    return pl.pallas_call(
        functools.partial(last_kernel, step=step, **options),
        out_shape=jax.ShapeDtypeStruct((3 * n, n), BF16),
        in_specs=specs,
        out_specs=vmem,
        scratch_shapes=[pltpu.VMEM((n, n), F32)] + scratch,
        compiler_params=params,
        cost_estimate=cost,
        name="sweep_last",
    )(gram, *after)


def column_kernel(*refs, pieces):
    fields = refs[:pieces]
    values_ref, lags_ref, out_ref = refs[pieces], refs[pieces + 1], refs[-1]
    step, planes_out, _ = out_ref.shape
    n = values_ref.shape[1]
    planes = lags_ref.shape[1]
    first = pl.program_id(0) * step
    for i in range(step):
        field = jnp.concatenate([f[i] for f in fields], axis=0)
        sums = lax.dot_general(
            field, values_ref[...], (((0,), (0,)), ((), ())), preferred_element_type=F32
        )
        high, low = split(sums * sums)
        row = jnp.broadcast_to(lags_ref[pl.ds(first + i, 1), :], (planes_out, planes))
        circ_high, circ_low = split(pltpu.roll(row, 0, 1, stride=1, stride_axis=0))
        circ = jnp.concatenate([circ_high, circ_low], axis=0)
        both = jnp.dot(
            jnp.concatenate([circ, circ], axis=1),
            jnp.concatenate([high, low], axis=0),
            preferred_element_type=F32,
        )
        w_high, w_low = split(both[:planes_out] + both[planes_out:])
        out_ref[i, :, :n] = w_high
        out_ref[i, :, n:] = w_low


def convolve(pieces, values, lags, planes_out, after):
    cols, _, planes = pieces[0].shape
    bands, n = values.shape
    step = 2
    return pl.pallas_call(
        functools.partial(column_kernel, pieces=len(pieces)),
        grid=(cols // step,),
        out_shape=jax.ShapeDtypeStruct((cols, planes_out, 2 * n), BF16),
        in_specs=[pl.BlockSpec((step, p.shape[1], planes), lambda j: (j, 0, 0)) for p in pieces]
        + [
            pl.BlockSpec((bands, n), lambda j: (0, 0)),
            pl.BlockSpec((cols, planes), lambda j: (0, 0)),
        ]
        + [pl.BlockSpec(memory_space=pl.ANY)] * len(after),
        out_specs=pl.BlockSpec((step, planes_out, 2 * n), lambda j: (j, 0, 0)),
        compiler_params=pltpu.CompilerParams(vmem_limit_bytes=40 * MIB),
        cost_estimate=pl.CostEstimate(
            flops=2 * cols * n * planes * (bands + 4 * planes_out),
            bytes_accessed=2 * cols * (bands * planes + 2 * planes_out * n),
            transcendentals=0,
        ),
        name="convolve",
    )(*pieces, values, lags, *after)


def fit_kernel(at_ref, w_ref, inverse_ref, *refs):
    out_ref = refs[-1]
    slab, cols, n = out_ref.shape
    w = w_ref[...].reshape(cols * slab, 2 * n)
    w = jnp.concatenate([w[:, :n], w[:, :n], w[:, n:]], axis=1)
    out = jnp.dot(w, inverse_ref[...], preferred_element_type=F32)
    out = jnp.swapaxes(out.reshape(cols, slab, n), 0, 1)
    out_ref[...] = out.astype(out_ref.dtype)


def fit(at, w, inverse, width, into=None):
    cols, planes_out, n2 = w.shape
    n = n2 // 2
    slab = planes_out // 2
    step = 16
    state = [] if into is None else [into]
    return pl.pallas_call(
        fit_kernel,
        grid_spec=pltpu.PrefetchScalarGridSpec(
            num_scalar_prefetch=1,
            grid=(cols // step,),
            in_specs=[
                pl.BlockSpec((step, slab, n2), lambda j, at: (j, at[0], 0)),
                pl.BlockSpec((3 * n, n), lambda j, at: (0, 0)),
            ]
            + [pl.BlockSpec(memory_space=pl.ANY)] * len(state),
            out_specs=pl.BlockSpec((slab, step, n), lambda j, at: (0, j + at[1], 0)),
        ),
        out_shape=jax.ShapeDtypeStruct((slab, width, n), BF16),
        input_output_aliases={3: 0} if state else {},
        compiler_params=pltpu.CompilerParams(vmem_limit_bytes=56 * MIB),
        cost_estimate=pl.CostEstimate(
            flops=6 * cols * slab * n * n,
            bytes_accessed=6 * cols * slab * n + 6 * n * n,
            transcendentals=0,
        ),
        name="fit",
    )(at, w, inverse, *state)


def per_device(orbitals, points, coulomb):
    gz_count = lax.axis_size("gz")
    gy_count = lax.axis_size("gy")
    gz = lax.axis_index("gz")
    gy = lax.axis_index("gy")
    bands_local, planes, columns = orbitals.shape
    n = points.shape[0]
    col_block = columns // gy_count
    half = col_block // 2
    slab = planes // gz_count
    pairs = gz_count // 2
    me = gz % 2
    pair = gz // 2
    chunks = 2
    chunk = half // chunks

    def hop(array, bit):
        return lax.ppermute(array, "gz", [(z, z ^ bit) for z in range(gz_count)])

    turned = jnp.transpose(orbitals, (2, 0, 1))
    blocks = turned.reshape(gy_count, 2, half, bands_local, planes)
    own = lax.dynamic_index_in_dim(blocks, me, 1, keepdims=False)
    partner = hop(lax.dynamic_index_in_dim(blocks, 1 - me, 1, keepdims=False), 1)

    local_values = take_points(points, turned.astype(F32), columns).astype(BF16)
    gathered = lax.all_gather(local_values, ("gz", "gy"), axis=0, tiled=True)
    zero = jnp.isnan(gathered[0, 0]).astype(jnp.int32)

    merged = jnp.concatenate([own, partner], axis=2)
    mine = []
    for c in range(chunks):
        parts = []
        for dg in range(gy_count):
            part = lax.dynamic_slice(
                merged,
                ((gy + dg + zero) % gy_count, c * chunk, 0, 0),
                (1, chunk, 2 * bands_local, planes),
            )[0]
            if dg:
                perm = [(y, (y + dg) % gy_count) for y in range(gy_count)]
                part = lax.ppermute(part, "gy", perm)
            parts.append(part)
        mine.append(jnp.concatenate(parts, axis=1))
    rows = mine[0].shape[1]

    pieces = []
    for c in range(chunks):
        if pairs == 4:
            first, second = hop(mine[c], 2), hop(mine[c], 4)
            pieces.append((first, second))
        else:
            groups = [[2 * p + e for p in range(pairs)] for e in range(2)]
            every = lax.all_gather(mine[c], "gz", axis=0, axis_index_groups=groups)
            pieces.append(tuple(every[p] for p in range(pairs)))
    relays = []
    for c in range(chunks):
        if pairs == 4:
            first, second = pieces[c]
            relays.append((hop(second[:, : rows // 2], 2), hop(first[:, rows // 2 :], 4)))
    if pairs == 4:
        order = jnp.arange(pairs, dtype=jnp.int32) ^ pair
        fields = [(mine[c],) + pieces[c] + relays[c] for c in range(chunks)]
        after = [(mine[0],), (mine[1],) + pieces[0], ()]
        after_columns = pieces[1]
    else:
        order = jnp.arange(pairs, dtype=jnp.int32)
        fields = pieces
        after = [(), (), ()]
        after_columns = ()

    slot_ids = jnp.arange(gy_count * 2, dtype=jnp.int32)
    from_gy = (gy - slot_ids // 2) % gy_count
    from_me = me ^ (slot_ids % 2)
    source = (2 * order[:, None] + from_me[None, :]) * gy_count + from_gy[None, :]
    ordered = jnp.take(
        gathered.reshape(-1, bands_local, n), source.reshape(-1), axis=0
    ).reshape(gathered.shape)

    steps = n // 256
    gram = sweep_gram(gathered, None, 0, ())
    for step in range(1, steps):
        gram = sweep_gram(gathered, gram, step, after[step - 1] if step <= 3 else ())
    inverse = gram

    grid = np.arange(planes, dtype=np.int64)
    table = np.cos((2.0 * np.pi / planes) * ((grid[:, None] * grid[None, :]) % planes))
    kernel = lax.dynamic_slice_in_dim(coulomb, me * half, half, 1).T
    lags = jnp.dot(
        kernel, jnp.asarray(table / planes, F32), precision=HIGH, preferred_element_type=F32
    )
    lags = jnp.roll(lags, pair * (2 * slab), axis=1)

    weights = [
        convolve(
            fields[c],
            ordered,
            lags[c * chunk : (c + 1) * chunk],
            2 * slab,
            after_columns if c == 0 else (),
        )
        for c in range(chunks)
    ]
    result = None
    arrived = []
    for c in range(chunks):
        zero_at = jnp.zeros((), jnp.int32)
        there = fit(jnp.stack([1 - me, zero_at]), weights[c], inverse, chunk)
        arrived.append(hop(there, 1))
        at = (me * half + c * chunk) // 16
        result = fit(jnp.stack([me, at]), weights[c], inverse, col_block, result)
    for c in range(chunks):
        result = lax.dynamic_update_slice(
            result, arrived[c], (0, (1 - me) * half + c * chunk, 0)
        )
    return result


def solution(mesh):
    return jax.shard_map(
        per_device,
        mesh=mesh,
        in_specs=(P(("gz", "gy"), None, None), P(), P(None, "gy")),
        out_specs=P("gz", "gy", None),
        check_vma=False,
    )
```

```python
import functools
import math

import jax
import jax.numpy as jnp
import numpy as np
from jax import lax
from jax.experimental import pallas as pl
from jax.experimental.pallas import tpu as pltpu
from jax.sharding import PartitionSpec as P

F32 = jnp.float32
BF16 = jnp.bfloat16
HIGH = lax.Precision.HIGHEST
MIB = 1024 * 1024


def split(value):
    high = value.astype(BF16)
    return high, (value - high.astype(F32)).astype(BF16)


def points_kernel(where_ref, field_ref, out_ref):
    bands = field_ref.shape[1]
    lane = lax.broadcasted_iota(jnp.int32, (bands, 128), 1)

    def tile(t, _):
        base = pl.multiple_of(t * 128, 128)

        def some(s, accs):
            accs = list(accs)
            for u in range(16):
                m = s * 16 + u
                column = where_ref[0, base + m]
                at = pl.multiple_of(where_ref[1, base + m], 128)
                row = field_ref[column, :, pl.ds(at, 128)]
                row = pltpu.roll(row, where_ref[2, base + m], 1)
                accs[u % 4] = jnp.where(lane == m, row, accs[u % 4])
            return tuple(accs)

        accs = lax.fori_loop(0, 8, some, (jnp.zeros((bands, 128), F32),) * 4)
        out_ref[:, pl.ds(base, 128)] = (accs[0] + accs[1]) + (accs[2] + accs[3])
        return 0

    lax.fori_loop(0, out_ref.shape[1] // 128, tile, 0)


def take_points(points, field, columns):
    plane = points // columns
    at = plane // 128 * 128
    shift = (jnp.arange(points.shape[0], dtype=jnp.int32) - plane) % 128
    where = jnp.stack([points - plane * columns, at, shift])
    return pl.pallas_call(
        points_kernel,
        out_shape=jax.ShapeDtypeStruct((field.shape[1], points.shape[0]), F32),
        in_specs=[
            pl.BlockSpec(memory_space=pltpu.SMEM),
            pl.BlockSpec(memory_space=pltpu.VMEM),
        ],
        out_specs=pl.BlockSpec(memory_space=pltpu.VMEM),
        compiler_params=pltpu.CompilerParams(vmem_limit_bytes=32 * MIB),
        name="take_points",
    )(where, field)


def sweep_small(a):
    n = a.shape[0]
    lane = lax.broadcasted_iota(jnp.int32, (8, n), 1)
    wide = lax.broadcasted_iota(jnp.int32, (n, n), 1)
    sub = lax.broadcasted_iota(jnp.int32, (8, n), 0)
    for g in range(n // 8):
        lo = 8 * g
        rows = a[lo : lo + 8, :]
        cols = [jnp.broadcast_to(a[:, lo + j : lo + j + 1], (n, n)) for j in range(8)]
        t = [c[lo : lo + 8, :] for c in cols]
        for k in range(8):
            pivot = jnp.broadcast_to(t[k][k : k + 1, :], (8, n))
            scale = pl.reciprocal(pivot, approx=True)
            scale = scale * (2.0 - pivot * scale)
            scale = scale * (2.0 - pivot * scale)
            here = sub == k
            new = []
            for j in range(8):
                if j == k:
                    new.append(jnp.where(here, -1.0, t[k]) * scale)
                else:
                    factor = jnp.broadcast_to(t[j][k : k + 1, :], (8, n))
                    kept = jnp.where(here, 0.0, t[j])
                    new.append(kept - (jnp.where(here, -1.0, t[k]) * factor) * scale)
            t = new
        terms = [t[j] * jnp.broadcast_to(rows[j : j + 1, :], (8, n)) for j in range(8)]
        while len(terms) > 1:
            terms = [x + y for x, y in zip(terms[::2], terms[1::2])]
        q = -terms[0]
        for j in range(8):
            q = jnp.where(lane == lo + j, t[j], q)
        inside = (wide >= lo) & (wide < lo + 8)
        terms = [cols[j] * jnp.broadcast_to(q[j : j + 1, :], (n, n)) for j in range(8)]
        while len(terms) > 1:
            terms = [x + y for x, y in zip(terms[::2], terms[1::2])]
        upd = jnp.where(inside, 0.0, a) - terms[0]
        a = jnp.concatenate(
            ([upd[:lo]] if lo else []) + [q] + ([upd[lo + 8 :]] if lo + 8 < n else []), axis=0
        )
    return a


def mm(a, b):
    return jnp.dot(a, b, precision=HIGH, preferred_element_type=F32)


def sweep_step(gram, block, panel, k, *, big, small):
    n = gram.shape[0]
    inner = lax.broadcasted_iota(jnp.int32, (small, big), 1)
    inner_full = lax.broadcasted_iota(jnp.int32, (big, big), 1)
    at = k * big
    kr = slice(at, at + big)
    block[...] = gram[kr, kr]
    for s in range(big // small):
        lo = s * small
        sr = slice(lo, lo + small)
        negative = sweep_small(block[sr, sr])
        q = -mm(negative, block[sr, :])
        inside = (inner >= lo) & (inner < lo + small)
        q = jnp.where(inside, jnp.concatenate([negative] * (big // small), axis=1), q)
        inside_full = (inner_full >= lo) & (inner_full < lo + small)
        upd = jnp.where(inside_full, 0.0, block[...]) - mm(block[:, sr], q)
        block[...] = upd
        block[sr, :] = q
    panel[...] = -mm(block[...], gram[kr, :])
    panel[:, kr] = block[...]
    wide = lax.broadcasted_iota(jnp.int32, (big, n), 1)
    inside = (wide >= at) & (wide < at + big)

    @pl.loop(0, n // big)
    def _(t):
        r = pl.ds(pl.multiple_of(t * big, big), big)
        col = gram[r, kr]
        gram[r, :] = jnp.where(inside, 0.0, gram[r, :]) - mm(col, panel[...])

    gram[kr, :] = panel[...]


def first_kernel(values_ref, gram, block, panel, *, big, small):
    @pl.loop(0, gram.shape[0] // big)
    def _(t):
        r = pl.ds(pl.multiple_of(t * big, big), big)
        base = lax.dot_general(
            values_ref[:, r], values_ref[...], (((0,), (0,)), ((), ())), preferred_element_type=F32
        )
        gram[r, :] = base * base

    sweep_step(gram, block, panel, 0, big=big, small=small)


def middle_kernel(*refs, step, big, small):
    gram, block, panel = refs[-3:]
    sweep_step(gram, block, panel, step, big=big, small=small)


def last_kernel(gram_ref, *refs, step, big, small):
    out_ref, gram, block, panel = refs[-4:]
    n = gram.shape[0]
    gram[...] = gram_ref[...]
    sweep_step(gram, block, panel, step, big=big, small=small)

    @pl.loop(0, n // big)
    def _(t):
        at = pl.multiple_of(t * big, big)
        high, low = split(-gram[pl.ds(at, big), :])
        out_ref[pl.ds(at, big), :] = high
        out_ref[pl.ds(at + n, big), :] = low


def sweep_gram(values, gram, step, after):
    big, small = 256, 128
    n = values.shape[1]
    last = step == n // big - 1
    vmem = pl.BlockSpec(memory_space=pltpu.VMEM)
    anywhere = pl.BlockSpec(memory_space=pl.ANY)
    state = jax.ShapeDtypeStruct((n, n), F32)
    scratch = [pltpu.VMEM((big, big), F32), pltpu.VMEM((big, n), F32)]
    options = dict(big=big, small=small)
    params = pltpu.CompilerParams(vmem_limit_bytes=24 * MIB)
    cost = pl.CostEstimate(flops=n * n, bytes_accessed=n * n, transcendentals=0)
    if step == 0:
        return pl.pallas_call(
            functools.partial(first_kernel, **options),
            out_shape=state,
            in_specs=[vmem],
            out_specs=vmem,
            scratch_shapes=scratch,
            compiler_params=params,
            cost_estimate=cost,
            name="sweep_first",
        )(values)
    specs = [vmem] + [anywhere] * len(after)
    if not last:
        return pl.pallas_call(
            functools.partial(middle_kernel, step=step, **options),
            out_shape=state,
            in_specs=specs,
            out_specs=vmem,
            scratch_shapes=scratch,
            input_output_aliases={0: 0},
            compiler_params=params,
            cost_estimate=cost,
            name="sweep_middle",
        )(gram, *after)
    return pl.pallas_call(
        functools.partial(last_kernel, step=step, **options),
        out_shape=jax.ShapeDtypeStruct((2 * n, n), BF16),
        in_specs=specs,
        out_specs=vmem,
        scratch_shapes=[pltpu.VMEM((n, n), F32)] + scratch,
        compiler_params=params,
        cost_estimate=cost,
        name="sweep_last",
    )(gram, *after)


def column_kernel(*refs, pieces):
    fields = refs[:pieces]
    values_ref, lags_ref, out_ref = refs[pieces], refs[pieces + 1], refs[-1]
    step, planes_out, _ = out_ref.shape
    n = values_ref.shape[1]
    planes = lags_ref.shape[1]
    first = pl.program_id(0) * step
    turned = [jnp.concatenate([f[i] for f in fields], axis=0).T for i in range(step)]
    sums = jnp.dot(
        jnp.concatenate(turned, axis=0), values_ref[...], preferred_element_type=F32
    )
    for i in range(step):
        mine = sums[i * planes : (i + 1) * planes]
        high, low = split(mine * mine)
        row = jnp.broadcast_to(lags_ref[pl.ds(first + i, 1), :], (planes_out, planes))
        circ_high, circ_low = split(pltpu.roll(row, 0, 1, stride=1, stride_axis=0))
        circ = jnp.concatenate([circ_high, circ_low], axis=0)
        both = jnp.dot(
            jnp.concatenate([circ, circ], axis=1),
            jnp.concatenate([high, low], axis=0),
            preferred_element_type=F32,
        )
        w_high, w_low = split(both[:planes_out] + both[planes_out:])
        out_ref[i, :, :n] = w_high
        out_ref[i, :, n:] = w_low


def convolve(pieces, values, lags, planes_out, start, state, after):
    cols, _, planes = pieces[0].shape
    all_cols = lags.shape[0]
    bands, n = values.shape
    step = 4
    extra = ([] if state is None else [state]) + list(after)
    return pl.pallas_call(
        functools.partial(column_kernel, pieces=len(pieces)),
        grid=(cols // step,),
        out_shape=jax.ShapeDtypeStruct((all_cols, planes_out, 2 * n), BF16),
        in_specs=[pl.BlockSpec((step, p.shape[1], planes), lambda j: (j, 0, 0)) for p in pieces]
        + [
            pl.BlockSpec((bands, n), lambda j: (0, 0)),
            pl.BlockSpec((cols, planes), lambda j: (start // cols, 0)),
        ]
        + [pl.BlockSpec(memory_space=pl.ANY)] * len(extra),
        out_specs=pl.BlockSpec((step, planes_out, 2 * n), lambda j: (j + start // step, 0, 0)),
        input_output_aliases={} if state is None else {len(pieces) + 2: 0},
        compiler_params=pltpu.CompilerParams(vmem_limit_bytes=40 * MIB),
        cost_estimate=pl.CostEstimate(
            flops=2 * cols * n * planes * (bands + 4 * planes_out),
            bytes_accessed=2 * cols * (bands * planes + 2 * planes_out * n),
            transcendentals=0,
        ),
        name="convolve",
    )(*pieces, values, lags, *extra)


def fit_kernel(at_ref, w_ref, inverse_ref, out_ref, turn):
    slab, cols, n = out_ref.shape
    w = w_ref[...].reshape(cols * slab, 2 * n)
    out = jnp.dot(w[:, :n], inverse_ref[:n], preferred_element_type=F32)
    out = out + jnp.dot(w[:, :n], inverse_ref[n:], preferred_element_type=F32)
    out = out + jnp.dot(w[:, n:], inverse_ref[:n], preferred_element_type=F32)
    for t in range(n // 128):
        lanes = slice(t * 128, (t + 1) * 128)
        for c in range(cols):
            turn[t, pl.ds(c, slab, stride=cols), :] = out[c * slab : (c + 1) * slab, lanes]
        out_ref[:, :, lanes] = turn[t].reshape(slab, cols, 128).astype(out_ref.dtype)


def fit(at, w, inverse, width):
    cols, planes_out, n2 = w.shape
    n = n2 // 2
    slab = planes_out // 2
    step = 16
    return pl.pallas_call(
        fit_kernel,
        grid_spec=pltpu.PrefetchScalarGridSpec(
            num_scalar_prefetch=1,
            grid=(cols // step,),
            in_specs=[
                pl.BlockSpec((step, slab, n2), lambda j, at: (j, at[0], 0)),
                pl.BlockSpec((2 * n, n), lambda j, at: (0, 0)),
            ],
            out_specs=pl.BlockSpec((slab, step, n), lambda j, at: (0, j + at[1], 0)),
            scratch_shapes=[pltpu.VMEM((n // 128, slab * step, 128), F32)],
        ),
        out_shape=jax.ShapeDtypeStruct((slab, width, n), BF16),
        compiler_params=pltpu.CompilerParams(vmem_limit_bytes=48 * MIB),
        cost_estimate=pl.CostEstimate(
            flops=6 * cols * slab * n * n,
            bytes_accessed=6 * cols * slab * n + 4 * n * n,
            transcendentals=0,
        ),
        name="fit",
    )(at, w, inverse)


def zero_after(array):
    return jnp.isnan(array[(0,) * array.ndim]).astype(jnp.int32)


def per_device(orbitals, points, coulomb):
    gz_count = lax.axis_size("gz")
    gy_count = lax.axis_size("gy")
    gz = lax.axis_index("gz")
    gy = lax.axis_index("gy")
    bands_local, planes, columns = orbitals.shape
    n = points.shape[0]
    col_block = columns // gy_count
    half = col_block // 2
    slab = planes // gz_count
    pairs = gz_count // 2
    me = gz % 2
    pair = gz // 2
    total_bands = bands_local * gz_count * gy_count
    chunks = 2
    chunk = half // chunks

    def hop(array, bit):
        return lax.ppermute(array, "gz", [(z, z ^ bit) for z in range(gz_count)])

    def wait_for(array, other):
        return jnp.where(zero_after(other) == 0, array, jnp.zeros_like(array))

    def relay(both, other):
        first, second = both
        first = wait_for(first[:, rows // 2 :], other)
        second = wait_for(second[:, : rows // 2], other)
        return hop(second, 2), hop(first, 4)

    def gy_shift(array, by):
        return lax.ppermute(array, "gy", [(y, (y + by) % gy_count) for y in range(gy_count)])

    turned = jnp.transpose(orbitals, (2, 0, 1))
    blocks = turned.reshape(gy_count, 2, half, bands_local, planes)
    own = lax.dynamic_index_in_dim(blocks, me, 1, keepdims=False)
    partner = hop(lax.dynamic_index_in_dim(blocks, 1 - me, 1, keepdims=False), 1)

    values = take_points(points, turned.astype(F32), columns).astype(BF16)
    values = jnp.concatenate([values, hop(values, 1)], axis=0)
    values = jnp.concatenate(
        [values] + [gy_shift(values, dg) for dg in range(1, gy_count)], axis=0
    )
    column_values = values
    values = jnp.concatenate(
        [values] + [hop(values, 2 * p) for p in range(1, pairs)], axis=0
    )
    zero = zero_after(column_values[-1:])

    merged = jnp.concatenate([own, partner], axis=2)
    arriving = []
    for c in range(chunks):
        arriving.append([])
        for dg in range(gy_count):
            part = lax.dynamic_slice(
                merged,
                ((gy + dg + zero) % gy_count, c * chunk, 0, 0),
                (1, chunk, 2 * bands_local, planes),
            )[0]
            arriving[c].append(gy_shift(part, dg) if dg else part)

    steps = n // 256
    gram = sweep_gram(values, None, 0, ())

    fields = [None] * chunks
    rows = total_bands // pairs
    pending = None
    for step in range(1, steps):
        after = ()
        if step <= chunks:
            c = step - 1
            mine = wait_for(jnp.concatenate(arriving[c], axis=1), gram)
            after = (mine,)
            if pairs == 4:
                if pending is not None:
                    after = after + pending
                    fields[c - 1] = fields[c - 1] + relay(pending, gram)
                pending = (hop(mine, 2), hop(mine, 4))
                fields[c] = (mine,) + pending
            else:
                fields[c] = (mine,) + tuple(hop(mine, 2 * p) for p in range(1, pairs))
        elif pending is not None:
            after = pending
            fields[chunks - 1] = fields[chunks - 1] + relay(pending, gram)
            pending = None
        gram = sweep_gram(values, gram, step, after)
    inverse = gram

    grid = np.arange(planes, dtype=np.int64)
    table = np.cos((2.0 * np.pi / planes) * ((grid[:, None] * grid[None, :]) % planes))
    kernel = lax.dynamic_slice_in_dim(coulomb, me * half, half, 1).T
    lags = jnp.dot(
        kernel, jnp.asarray(table / planes, F32), precision=HIGH, preferred_element_type=F32
    )
    lags = jnp.roll(lags, pair * (2 * slab), axis=1)

    weights = None
    for c in range(chunks):
        weights = convolve(fields[c], values, lags, 2 * slab, c * chunk, weights, ())
    there = fit(jnp.stack([1 - me, jnp.zeros((), jnp.int32)]), weights, inverse, half)
    there = hop(there, 1)
    result = fit(jnp.stack([me, me * half // 16]), weights, inverse, col_block)
    return lax.dynamic_update_slice(result, there, (0, (1 - me) * half, 0))


def solution(mesh):
    return jax.shard_map(
        per_device,
        mesh=mesh,
        in_specs=(P(("gz", "gy"), None, None), P(), P(None, "gy")),
        out_specs=P("gz", "gy", None),
        check_vma=False,
    )
```

```python
import functools
import math

import jax
import jax.numpy as jnp
import numpy as np
from jax import lax
from jax.experimental import pallas as pl
from jax.experimental.pallas import tpu as pltpu
from jax.sharding import PartitionSpec as P

F32 = jnp.float32
BF16 = jnp.bfloat16
HIGH = lax.Precision.HIGHEST
MIB = 1024 * 1024


def split(value):
    high = value.astype(BF16)
    return high, (value - high.astype(F32)).astype(BF16)


def points_kernel(where_ref, field_ref, out_ref):
    bands = field_ref.shape[1]
    lane = lax.broadcasted_iota(jnp.int32, (bands, 128), 1)

    def tile(t, _):
        base = pl.multiple_of(t * 128, 128)

        def some(s, accs):
            accs = list(accs)
            first = s * 32
            late = lane - first
            for u in range(32):
                m = first + u
                column = where_ref[0, base + m]
                at = pl.multiple_of(where_ref[1, base + m], 128)
                row = field_ref[column, :, pl.ds(at, 128)]
                row = pltpu.roll(row, where_ref[2, base + m], 1)
                accs[u % 4] = jnp.where(late == u, row, accs[u % 4])
            return tuple(accs)

        accs = lax.fori_loop(0, 4, some, (jnp.zeros((bands, 128), F32),) * 4)
        out_ref[:, pl.ds(base, 128)] = (accs[0] + accs[1]) + (accs[2] + accs[3])
        return 0

    lax.fori_loop(0, out_ref.shape[1] // 128, tile, 0)


def take_points(points, field, columns):
    plane = points // columns
    at = plane // 128 * 128
    shift = (jnp.arange(points.shape[0], dtype=jnp.int32) - plane) % 128
    where = jnp.stack([points - plane * columns, at, shift])
    return pl.pallas_call(
        points_kernel,
        out_shape=jax.ShapeDtypeStruct((field.shape[1], points.shape[0]), F32),
        in_specs=[
            pl.BlockSpec(memory_space=pltpu.SMEM),
            pl.BlockSpec(memory_space=pltpu.VMEM),
        ],
        out_specs=pl.BlockSpec(memory_space=pltpu.VMEM),
        compiler_params=pltpu.CompilerParams(vmem_limit_bytes=32 * MIB),
        name="take_points",
    )(where, field)


def sweep_small(a):
    n = a.shape[0]
    lane = lax.broadcasted_iota(jnp.int32, (8, n), 1)
    wide = lax.broadcasted_iota(jnp.int32, (n, n), 1)
    sub = lax.broadcasted_iota(jnp.int32, (8, n), 0)
    for g in range(n // 8):
        lo = 8 * g
        rows = a[lo : lo + 8, :]
        cols = [jnp.broadcast_to(a[:, lo + j : lo + j + 1], (n, n)) for j in range(8)]
        t = [c[lo : lo + 8, :] for c in cols]
        for k in range(8):
            pivot = jnp.broadcast_to(t[k][k : k + 1, :], (8, n))
            scale = 1.0 / pivot
            here = sub == k
            new = []
            for j in range(8):
                if j == k:
                    new.append(jnp.where(here, -1.0, t[k]) * scale)
                else:
                    factor = jnp.broadcast_to(t[j][k : k + 1, :], (8, n))
                    kept = jnp.where(here, 0.0, t[j])
                    new.append(kept - (jnp.where(here, -1.0, t[k]) * factor) * scale)
            t = new
        terms = [t[j] * jnp.broadcast_to(rows[j : j + 1, :], (8, n)) for j in range(8)]
        while len(terms) > 1:
            terms = [x + y for x, y in zip(terms[::2], terms[1::2])]
        q = -terms[0]
        for j in range(8):
            q = jnp.where(lane == lo + j, t[j], q)
        inside = (wide >= lo) & (wide < lo + 8)
        terms = [cols[j] * jnp.broadcast_to(q[j : j + 1, :], (n, n)) for j in range(8)]
        while len(terms) > 1:
            terms = [x + y for x, y in zip(terms[::2], terms[1::2])]
        upd = jnp.where(inside, 0.0, a) - terms[0]
        a = jnp.concatenate(
            ([upd[:lo]] if lo else []) + [q] + ([upd[lo + 8 :]] if lo + 8 < n else []), axis=0
        )
    return a


def mm(a, b):
    return jnp.dot(a, b, precision=HIGH, preferred_element_type=F32)


def sweep_step(gram, block, panel, k, *, big, small):
    n = gram.shape[0]
    inner = lax.broadcasted_iota(jnp.int32, (small, big), 1)
    inner_full = lax.broadcasted_iota(jnp.int32, (big, big), 1)
    at = k * big
    kr = slice(at, at + big)
    block[...] = gram[kr, kr]
    for s in range(big // small):
        lo = s * small
        sr = slice(lo, lo + small)
        negative = sweep_small(block[sr, sr])
        q = -mm(negative, block[sr, :])
        inside = (inner >= lo) & (inner < lo + small)
        q = jnp.where(inside, jnp.concatenate([negative] * (big // small), axis=1), q)
        inside_full = (inner_full >= lo) & (inner_full < lo + small)
        upd = jnp.where(inside_full, 0.0, block[...]) - mm(block[:, sr], q)
        block[...] = upd
        block[sr, :] = q
    panel[...] = -mm(block[...], gram[kr, :])
    panel[:, kr] = block[...]
    wide = lax.broadcasted_iota(jnp.int32, (big, n), 1)
    inside = (wide >= at) & (wide < at + big)

    @pl.loop(0, n // big)
    def _(t):
        r = pl.ds(pl.multiple_of(t * big, big), big)
        col = gram[r, kr]
        gram[r, :] = jnp.where(inside, 0.0, gram[r, :]) - mm(col, panel[...])

    gram[kr, :] = panel[...]


def first_kernel(values_ref, gram, block, panel, *, big, small):
    @pl.loop(0, gram.shape[0] // big)
    def _(t):
        r = pl.ds(pl.multiple_of(t * big, big), big)
        base = lax.dot_general(
            values_ref[:, r], values_ref[...], (((0,), (0,)), ((), ())), preferred_element_type=F32
        )
        gram[r, :] = base * base

    sweep_step(gram, block, panel, 0, big=big, small=small)


def middle_kernel(*refs, step, big, small):
    gram, block, panel = refs[-3:]
    sweep_step(gram, block, panel, step, big=big, small=small)


def last_kernel(gram_ref, *refs, step, big, small):
    out_ref, gram, block, panel = refs[-4:]
    n = gram.shape[0]
    gram[...] = gram_ref[...]
    sweep_step(gram, block, panel, step, big=big, small=small)

    @pl.loop(0, n // big)
    def _(t):
        at = pl.multiple_of(t * big, big)
        high, low = split(-gram[pl.ds(at, big), :])
        out_ref[pl.ds(at, big), :] = high
        out_ref[pl.ds(at + n, big), :] = low


def sweep_gram(values, gram, step, after):
    big, small = 256, 128
    n = values.shape[1]
    last = step == n // big - 1
    vmem = pl.BlockSpec(memory_space=pltpu.VMEM)
    anywhere = pl.BlockSpec(memory_space=pl.ANY)
    state = jax.ShapeDtypeStruct((n, n), F32)
    scratch = [pltpu.VMEM((big, big), F32), pltpu.VMEM((big, n), F32)]
    options = dict(big=big, small=small)
    params = pltpu.CompilerParams(vmem_limit_bytes=16 * MIB)
    cost = pl.CostEstimate(flops=n * n, bytes_accessed=n * n, transcendentals=0)
    if step == 0:
        return pl.pallas_call(
            functools.partial(first_kernel, **options),
            out_shape=state,
            in_specs=[vmem],
            out_specs=vmem,
            scratch_shapes=scratch,
            compiler_params=params,
            cost_estimate=cost,
            name="sweep_first",
        )(values)
    specs = [vmem] + [anywhere] * len(after)
    if not last:
        return pl.pallas_call(
            functools.partial(middle_kernel, step=step, **options),
            out_shape=state,
            in_specs=specs,
            out_specs=vmem,
            scratch_shapes=scratch,
            input_output_aliases={0: 0},
            compiler_params=params,
            cost_estimate=cost,
            name="sweep_middle",
        )(gram, *after)
    return pl.pallas_call(
        functools.partial(last_kernel, step=step, **options),
        out_shape=jax.ShapeDtypeStruct((2 * n, n), BF16),
        in_specs=specs,
        out_specs=vmem,
        scratch_shapes=[pltpu.VMEM((n, n), F32)] + scratch,
        compiler_params=params,
        cost_estimate=cost,
        name="sweep_last",
    )(gram, *after)


def column_kernel(*refs, pieces):
    fields = refs[:pieces]
    values_ref, lags_ref, own_ref, other_ref = refs[pieces], refs[pieces + 1], refs[-2], refs[-1]
    step, slab, _ = own_ref.shape
    n = values_ref.shape[1]
    planes = lags_ref.shape[2]
    first = pl.program_id(0) * step
    turned = [jnp.concatenate([f[i] for f in fields], axis=0).T for i in range(step)]
    sums = jnp.dot(
        jnp.concatenate(turned, axis=0), values_ref[...], preferred_element_type=F32
    )
    for i in range(step):
        mine = sums[i * planes : (i + 1) * planes]
        high, low = split(mine * mine)
        circ = []
        for whose in range(2):
            row = jnp.broadcast_to(lags_ref[whose, pl.ds(first + i, 1), :], (slab, planes))
            circ.append(pltpu.roll(row, 0, 1, stride=1, stride_axis=0))
        circ = jnp.concatenate(split(jnp.concatenate(circ, axis=0)), axis=0)
        both = jnp.dot(
            jnp.concatenate([circ, circ], axis=1),
            jnp.concatenate([high, low], axis=0),
            preferred_element_type=F32,
        )
        w_high, w_low = split(both[: 2 * slab] + both[2 * slab :])
        own_ref[i, :, :n] = w_high[:slab]
        own_ref[i, :, n:] = w_low[:slab]
        other_ref[i, :, :n] = w_high[slab:]
        other_ref[i, :, n:] = w_low[slab:]


def convolve(pieces, values, lags, slab, start, state, after):
    cols, _, planes = pieces[0].shape
    all_cols = lags.shape[1]
    bands, n = values.shape
    step = 4
    shape = jax.ShapeDtypeStruct((all_cols, slab, 2 * n), BF16)
    out_spec = pl.BlockSpec((step, slab, 2 * n), lambda j: (j + start // step, 0, 0))
    return pl.pallas_call(
        functools.partial(column_kernel, pieces=len(pieces)),
        grid=(cols // step,),
        out_shape=(shape, shape),
        in_specs=[pl.BlockSpec((step, p.shape[1], planes), lambda j: (j, 0, 0)) for p in pieces]
        + [
            pl.BlockSpec((bands, n), lambda j: (0, 0)),
            pl.BlockSpec((2, cols, planes), lambda j: (0, start // cols, 0)),
        ]
        + [pl.BlockSpec(memory_space=pl.ANY)] * (len(state) + len(after)),
        out_specs=(out_spec, out_spec),
        input_output_aliases={len(pieces) + 2 + i: i for i in range(len(state))},
        compiler_params=pltpu.CompilerParams(vmem_limit_bytes=28 * MIB),
        cost_estimate=pl.CostEstimate(
            flops=2 * cols * n * planes * (bands + 8 * slab),
            bytes_accessed=2 * cols * (bands * planes + 4 * slab * n),
            transcendentals=0,
        ),
        name="convolve",
    )(*pieces, values, lags, *state, *after)


def fit_kernel(at_ref, w_ref, inverse_ref, *refs):
    out_ref, turn = refs[-2:]
    slab, cols, n = out_ref.shape
    w = w_ref[...].reshape(cols * slab, 2 * n)
    w_high, w_low = w[:, :n], w[:, n:]
    tile = 256
    for first in range(0, n, tile):
        lanes = slice(first, first + tile)
        high = inverse_ref[:n, lanes]
        out = jnp.dot(w_high, high, preferred_element_type=F32)
        out = out + jnp.dot(w_high, inverse_ref[n:, lanes], preferred_element_type=F32)
        out = out + jnp.dot(w_low, high, preferred_element_type=F32)
        for t in range(tile // 128):
            at = first // 128 + t
            part = slice(t * 128, (t + 1) * 128)
            for c in range(cols):
                turn[at, pl.ds(c, slab, stride=cols), :] = out[c * slab : (c + 1) * slab, part]
            out_ref[:, :, at * 128 : (at + 1) * 128] = (
                turn[at].reshape(slab, cols, 128).astype(out_ref.dtype)
            )


def fit(at, w, inverse, width, state):
    cols, slab, n2 = w.shape
    n = n2 // 2
    step = 16
    return pl.pallas_call(
        fit_kernel,
        grid_spec=pltpu.PrefetchScalarGridSpec(
            num_scalar_prefetch=1,
            grid=(cols // step,),
            in_specs=[
                pl.BlockSpec((step, slab, n2), lambda j, at: (j, 0, 0)),
                pl.BlockSpec((2 * n, n), lambda j, at: (0, 0)),
            ]
            + [pl.BlockSpec(memory_space=pl.ANY)] * len(state),
            out_specs=pl.BlockSpec((slab, step, n), lambda j, at: (0, j + at[0], 0)),
            scratch_shapes=[pltpu.VMEM((n // 128, slab * step, 128), F32)],
        ),
        out_shape=jax.ShapeDtypeStruct((slab, width, n), BF16),
        input_output_aliases={3: 0} if state else {},
        compiler_params=pltpu.CompilerParams(vmem_limit_bytes=32 * MIB),
        cost_estimate=pl.CostEstimate(
            flops=6 * cols * slab * n * n,
            bytes_accessed=6 * cols * slab * n + 4 * n * n,
            transcendentals=0,
        ),
        name="fit",
    )(at, w, inverse, *state)


def zero_after(array):
    return jnp.isnan(array[(0,) * array.ndim]).astype(jnp.int32)


def per_device(orbitals, points, coulomb):
    gz_count = lax.axis_size("gz")
    gy_count = lax.axis_size("gy")
    gz = lax.axis_index("gz")
    gy = lax.axis_index("gy")
    bands_local, planes, columns = orbitals.shape
    n = points.shape[0]
    col_block = columns // gy_count
    half = col_block // 2
    slab = planes // gz_count
    pairs = gz_count // 2
    me = gz % 2
    total_bands = bands_local * gz_count * gy_count
    chunks = 2
    chunk = half // chunks

    def hop(array, bit):
        return lax.ppermute(array, "gz", [(z, z ^ bit) for z in range(gz_count)])

    def wait_for(array, other):
        return jnp.where(zero_after(other) == 0, array, jnp.zeros_like(array))

    def relay(both, other):
        first, second = both
        first = wait_for(first[:, rows // 2 :], other)
        second = wait_for(second[:, : rows // 2], other)
        return hop(second, 2), hop(first, 4)

    def gy_shift(array, by):
        return lax.ppermute(array, "gy", [(y, (y + by) % gy_count) for y in range(gy_count)])

    turned = jnp.transpose(orbitals, (2, 0, 1))
    blocks = turned.reshape(gy_count, 2, half, bands_local, planes)
    own = lax.dynamic_index_in_dim(blocks, me, 1, keepdims=False)
    partner = hop(lax.dynamic_index_in_dim(blocks, 1 - me, 1, keepdims=False), 1)

    values = take_points(points, turned.astype(F32), columns).astype(BF16)
    values = jnp.concatenate([values, hop(values, 1)], axis=0)
    values = jnp.concatenate(
        [values] + [gy_shift(values, dg) for dg in range(1, gy_count)], axis=0
    )
    column_values = values
    values = jnp.concatenate(
        [values] + [hop(values, 2 * p) for p in range(1, pairs)], axis=0
    )
    zero = zero_after(column_values[-1:])

    merged = jnp.concatenate([own, partner], axis=2)
    arriving = []
    for c in range(chunks):
        arriving.append([])
        for dg in range(gy_count):
            part = lax.dynamic_slice(
                merged,
                ((gy + dg + zero) % gy_count, c * chunk, 0, 0),
                (1, chunk, 2 * bands_local, planes),
            )[0]
            arriving[c].append(gy_shift(part, dg) if dg else part)

    steps = n // 256
    gram = sweep_gram(values, None, 0, ())

    fields = [None] * chunks
    rows = total_bands // pairs
    pending = None
    for step in range(1, steps):
        after = ()
        if step <= chunks:
            c = step - 1
            mine = wait_for(jnp.concatenate(arriving[c], axis=1), gram)
            after = (mine,)
            if pairs == 4:
                if pending is not None:
                    after = after + pending
                    fields[c - 1] = fields[c - 1] + relay(pending, gram)
                pending = (hop(mine, 2), hop(mine, 4))
                fields[c] = (mine,) + pending
            else:
                fields[c] = (mine,) + tuple(hop(mine, 2 * p) for p in range(1, pairs))
        elif pending is not None:
            after = pending
            fields[chunks - 1] = fields[chunks - 1] + relay(pending, gram)
            pending = None
        gram = sweep_gram(values, gram, step, after)
    inverse = gram

    grid = np.arange(planes, dtype=np.int64)
    table = np.cos((2.0 * np.pi / planes) * ((grid[:, None] * grid[None, :]) % planes))
    kernel = lax.dynamic_slice_in_dim(coulomb, me * half, half, 1).T
    lags = jnp.dot(
        kernel, jnp.asarray(table / planes, F32), precision=HIGH, preferred_element_type=F32
    )
    lags = jnp.stack([jnp.roll(lags, z * slab, axis=1) for z in (gz, gz ^ 1)])

    weights = ()
    for c in range(chunks):
        after = (inverse,) if c else ()
        weights = convolve(fields[c], values, lags, slab, c * chunk, weights, after)
    own_weights, other_weights = weights
    other_weights = hop(other_weights, 1)
    blocks_of_16 = half // 16
    result = fit((me * blocks_of_16)[None], own_weights, inverse, col_block, ())
    return fit(((1 - me) * blocks_of_16)[None], other_weights, inverse, col_block, (result,))


def solution(mesh):
    return jax.shard_map(
        per_device,
        mesh=mesh,
        in_specs=(P(("gz", "gy"), None, None), P(), P(None, "gy")),
        out_specs=P("gz", "gy", None),
        check_vma=False,
    )
```

```python
import functools
import math

import jax
import jax.numpy as jnp
import numpy as np
from jax import lax
from jax.experimental import pallas as pl
from jax.experimental.pallas import tpu as pltpu
from jax.sharding import PartitionSpec as P

F32 = jnp.float32
BF16 = jnp.bfloat16
HIGH = lax.Precision.HIGHEST
MIB = 1024 * 1024


def split(value):
    high = value.astype(BF16)
    return high, (value - high.astype(F32)).astype(BF16)


def points_kernel(where_ref, field_ref, out_ref):
    bands = field_ref.shape[1]
    lane = lax.broadcasted_iota(jnp.int32, (bands, 128), 1)

    def tile(t, _):
        base = pl.multiple_of(t * 128, 128)

        def some(s, accs):
            accs = list(accs)
            first = s * 32
            late = lane - first
            for u in range(32):
                m = first + u
                column = where_ref[0, base + m]
                at = pl.multiple_of(where_ref[1, base + m], 128)
                row = field_ref[column, :, pl.ds(at, 128)]
                row = pltpu.roll(row, where_ref[2, base + m], 1)
                accs[u % 4] = jnp.where(late == u, row, accs[u % 4])
            return tuple(accs)

        accs = lax.fori_loop(0, 4, some, (jnp.zeros((bands, 128), F32),) * 4)
        out_ref[:, pl.ds(base, 128)] = (accs[0] + accs[1]) + (accs[2] + accs[3])
        return 0

    lax.fori_loop(0, out_ref.shape[1] // 128, tile, 0)


def take_points(points, field, columns):
    plane = points // columns
    at = plane // 128 * 128
    shift = (jnp.arange(points.shape[0], dtype=jnp.int32) - plane) % 128
    where = jnp.stack([points - plane * columns, at, shift])
    return pl.pallas_call(
        points_kernel,
        out_shape=jax.ShapeDtypeStruct((field.shape[1], points.shape[0]), F32),
        in_specs=[
            pl.BlockSpec(memory_space=pltpu.SMEM),
            pl.BlockSpec(memory_space=pltpu.VMEM),
        ],
        out_specs=pl.BlockSpec(memory_space=pltpu.VMEM),
        compiler_params=pltpu.CompilerParams(vmem_limit_bytes=32 * MIB),
        name="take_points",
    )(where, field)


def total(terms):
    while len(terms) > 1:
        terms = [x + y for x, y in zip(terms[::2], terms[1::2])]
    return terms[0]


def sweep_small(a):
    n = a.shape[0]
    lane = lax.broadcasted_iota(jnp.int32, (8, n), 1)
    wide = lax.broadcasted_iota(jnp.int32, (n, n), 1)
    sub = lax.broadcasted_iota(jnp.int32, (8, n), 0)

    def spread(x, row):
        return jnp.broadcast_to(x[row : row + 1, :], (8, n))

    t = [jnp.broadcast_to(a[:8, j : j + 1], (8, n)) for j in range(8)]
    for g in range(n // 8):
        lo = 8 * g
        to = lo + 8
        rows = a[lo:to, :]
        cols = [jnp.broadcast_to(a[:, lo + j : lo + j + 1], (n, n)) for j in range(8)]
        for k in range(8):
            scale = 1.0 / spread(t[k], k)
            here = sub == k
            new = []
            for j in range(8):
                if j == k:
                    new.append(jnp.where(here, -1.0, t[k]) * scale)
                else:
                    kept = jnp.where(here, 0.0, t[j])
                    new.append(kept - (jnp.where(here, -1.0, t[k]) * spread(t[j], k)) * scale)
            t = new
        swept = t
        if to < n:
            near = [c[to : to + 8, :] for c in cols]
            t = []
            for j in range(8):
                held = jnp.broadcast_to(a[to : to + 8, to + j : to + j + 1], (8, n))
                part = total([swept[m] * spread(near[m], j) for m in range(8)])
                t.append(held + total([near[k] * spread(part, k) for k in range(8)]))
        q = -total([swept[j] * spread(rows, j) for j in range(8)])
        for j in range(8):
            q = jnp.where(lane == lo + j, swept[j], q)
        inside = (wide >= lo) & (wide < to)
        upd = jnp.where(inside, 0.0, a) - total(
            [cols[j] * jnp.broadcast_to(q[j : j + 1, :], (n, n)) for j in range(8)]
        )
        a = jnp.concatenate(([upd[:lo]] if lo else []) + [q] + ([upd[to:]] if to < n else []), axis=0)
    return a


def mm(a, b):
    return jnp.dot(a, b, precision=HIGH, preferred_element_type=F32)


def sweep_step(gram, block, panel, k, *, big, small):
    n = gram.shape[0]
    inner = lax.broadcasted_iota(jnp.int32, (small, big), 1)
    inner_full = lax.broadcasted_iota(jnp.int32, (big, big), 1)
    at = k * big
    kr = slice(at, at + big)
    block[...] = gram[kr, kr]
    for s in range(big // small):
        lo = s * small
        sr = slice(lo, lo + small)
        negative = sweep_small(block[sr, sr])
        q = -mm(negative, block[sr, :])
        inside = (inner >= lo) & (inner < lo + small)
        q = jnp.where(inside, jnp.concatenate([negative] * (big // small), axis=1), q)
        inside_full = (inner_full >= lo) & (inner_full < lo + small)
        upd = jnp.where(inside_full, 0.0, block[...]) - mm(block[:, sr], q)
        block[...] = upd
        block[sr, :] = q
    panel[...] = -mm(block[...], gram[kr, :])
    panel[:, kr] = block[...]
    wide = lax.broadcasted_iota(jnp.int32, (big, n), 1)
    inside = (wide >= at) & (wide < at + big)

    @pl.loop(0, n // big)
    def _(t):
        r = pl.ds(pl.multiple_of(t * big, big), big)
        col = gram[r, kr]
        gram[r, :] = jnp.where(inside, 0.0, gram[r, :]) - mm(col, panel[...])

    gram[kr, :] = panel[...]


def first_kernel(values_ref, gram, block, panel, *, big, small):
    @pl.loop(0, gram.shape[0] // big)
    def _(t):
        r = pl.ds(pl.multiple_of(t * big, big), big)
        base = lax.dot_general(
            values_ref[:, r], values_ref[...], (((0,), (0,)), ((), ())), preferred_element_type=F32
        )
        gram[r, :] = base * base

    sweep_step(gram, block, panel, 0, big=big, small=small)


def middle_kernel(*refs, step, big, small):
    gram, block, panel = refs[-3:]
    sweep_step(gram, block, panel, step, big=big, small=small)


def last_kernel(gram_ref, *refs, step, big, small):
    out_ref, gram, block, panel = refs[-4:]
    n = gram.shape[0]
    gram[...] = gram_ref[...]
    sweep_step(gram, block, panel, step, big=big, small=small)

    @pl.loop(0, n // big)
    def _(t):
        at = pl.multiple_of(t * big, big)
        high, low = split(-gram[pl.ds(at, big), :])
        out_ref[pl.ds(at, big), :] = high
        out_ref[pl.ds(at + n, big), :] = low


def sweep_gram(values, gram, step, after):
    big, small = 256, 128
    n = values.shape[1]
    last = step == n // big - 1
    vmem = pl.BlockSpec(memory_space=pltpu.VMEM)
    anywhere = pl.BlockSpec(memory_space=pl.ANY)
    state = jax.ShapeDtypeStruct((n, n), F32)
    scratch = [pltpu.VMEM((big, big), F32), pltpu.VMEM((big, n), F32)]
    options = dict(big=big, small=small)
    params = pltpu.CompilerParams(vmem_limit_bytes=16 * MIB)
    cost = pl.CostEstimate(flops=n * n, bytes_accessed=n * n, transcendentals=0)
    if step == 0:
        return pl.pallas_call(
            functools.partial(first_kernel, **options),
            out_shape=state,
            in_specs=[vmem],
            out_specs=vmem,
            scratch_shapes=scratch,
            compiler_params=params,
            cost_estimate=cost,
            name="sweep_first",
        )(values)
    specs = [vmem] + [anywhere] * len(after)
    if not last:
        return pl.pallas_call(
            functools.partial(middle_kernel, step=step, **options),
            out_shape=state,
            in_specs=specs,
            out_specs=vmem,
            scratch_shapes=scratch,
            input_output_aliases={0: 0},
            compiler_params=params,
            cost_estimate=cost,
            name="sweep_middle",
        )(gram, *after)
    return pl.pallas_call(
        functools.partial(last_kernel, step=step, **options),
        out_shape=jax.ShapeDtypeStruct((2 * n, n), BF16),
        in_specs=specs,
        out_specs=vmem,
        scratch_shapes=[pltpu.VMEM((n, n), F32)] + scratch,
        compiler_params=params,
        cost_estimate=cost,
        name="sweep_last",
    )(gram, *after)


def column_kernel(*refs, pieces):
    fields = refs[:pieces]
    values_ref, lags_ref, own_ref, other_ref = refs[pieces], refs[pieces + 1], refs[-2], refs[-1]
    step, slab, _ = own_ref.shape
    n = values_ref.shape[1]
    planes = lags_ref.shape[2]
    first = pl.program_id(0) * step
    turned = [jnp.concatenate([f[i] for f in fields], axis=0).T for i in range(step)]
    sums = jnp.dot(
        jnp.concatenate(turned, axis=0), values_ref[...], preferred_element_type=F32
    )
    for i in range(step):
        mine = sums[i * planes : (i + 1) * planes]
        high, low = split(mine * mine)
        circ = []
        for whose in range(2):
            row = jnp.broadcast_to(lags_ref[whose, pl.ds(first + i, 1), :], (slab, planes))
            circ.append(pltpu.roll(row, 0, 1, stride=1, stride_axis=0))
        circ = jnp.concatenate(split(jnp.concatenate(circ, axis=0)), axis=0)
        both = jnp.dot(
            jnp.concatenate([circ, circ], axis=1),
            jnp.concatenate([high, low], axis=0),
            preferred_element_type=F32,
        )
        w_high, w_low = split(both[: 2 * slab] + both[2 * slab :])
        own_ref[i, :, :n] = w_high[:slab]
        own_ref[i, :, n:] = w_low[:slab]
        other_ref[i, :, :n] = w_high[slab:]
        other_ref[i, :, n:] = w_low[slab:]


def convolve(pieces, values, lags, slab, start, state, after):
    cols, _, planes = pieces[0].shape
    all_cols = lags.shape[1]
    bands, n = values.shape
    step = 4
    shape = jax.ShapeDtypeStruct((all_cols, slab, 2 * n), BF16)
    out_spec = pl.BlockSpec((step, slab, 2 * n), lambda j: (j + start // step, 0, 0))
    return pl.pallas_call(
        functools.partial(column_kernel, pieces=len(pieces)),
        grid=(cols // step,),
        out_shape=(shape, shape),
        in_specs=[pl.BlockSpec((step, p.shape[1], planes), lambda j: (j, 0, 0)) for p in pieces]
        + [
            pl.BlockSpec((bands, n), lambda j: (0, 0)),
            pl.BlockSpec((2, cols, planes), lambda j: (0, start // cols, 0)),
        ]
        + [pl.BlockSpec(memory_space=pl.ANY)] * (len(state) + len(after)),
        out_specs=(out_spec, out_spec),
        input_output_aliases={len(pieces) + 2 + i: i for i in range(len(state))},
        compiler_params=pltpu.CompilerParams(vmem_limit_bytes=48 * MIB),
        cost_estimate=pl.CostEstimate(
            flops=2 * cols * n * planes * (bands + 8 * slab),
            bytes_accessed=2 * cols * (bands * planes + 4 * slab * n),
            transcendentals=0,
        ),
        name="convolve",
    )(*pieces, values, lags, *state, *after)


def fit_kernel(at_ref, w_ref, inverse_ref, *refs):
    out_ref, turn = refs[-2:]
    slab, cols, n = out_ref.shape
    w = w_ref[...].reshape(cols * slab, 2 * n)
    w_high, w_low = w[:, :n], w[:, n:]
    tile = 256
    for first in range(0, n, tile):
        lanes = slice(first, first + tile)
        high = inverse_ref[:n, lanes]
        out = jnp.dot(w_high, high, preferred_element_type=F32)
        out = out + jnp.dot(w_high, inverse_ref[n:, lanes], preferred_element_type=F32)
        out = out + jnp.dot(w_low, high, preferred_element_type=F32)
        for t in range(tile // 128):
            at = first // 128 + t
            part = slice(t * 128, (t + 1) * 128)
            for c in range(cols):
                turn[at, pl.ds(c, slab, stride=cols), :] = out[c * slab : (c + 1) * slab, part]
            out_ref[:, :, at * 128 : (at + 1) * 128] = (
                turn[at].reshape(slab, cols, 128).astype(out_ref.dtype)
            )


def fit(at, w, inverse, width, state):
    cols, slab, n2 = w.shape
    n = n2 // 2
    step = 16
    return pl.pallas_call(
        fit_kernel,
        grid_spec=pltpu.PrefetchScalarGridSpec(
            num_scalar_prefetch=1,
            grid=(cols // step,),
            in_specs=[
                pl.BlockSpec((step, slab, n2), lambda j, at: (j, 0, 0)),
                pl.BlockSpec((2 * n, n), lambda j, at: (0, 0)),
            ]
            + [pl.BlockSpec(memory_space=pl.ANY)] * len(state),
            out_specs=pl.BlockSpec((slab, step, n), lambda j, at: (0, j + at[0], 0)),
            scratch_shapes=[pltpu.VMEM((n // 128, slab * step, 128), F32)],
        ),
        out_shape=jax.ShapeDtypeStruct((slab, width, n), BF16),
        input_output_aliases={3: 0} if state else {},
        compiler_params=pltpu.CompilerParams(vmem_limit_bytes=56 * MIB),
        cost_estimate=pl.CostEstimate(
            flops=6 * cols * slab * n * n,
            bytes_accessed=6 * cols * slab * n + 4 * n * n,
            transcendentals=0,
        ),
        name="fit",
    )(at, w, inverse, *state)


def zero_after(array):
    return jnp.isnan(array[(0,) * array.ndim]).astype(jnp.int32)


def per_device(orbitals, points, coulomb):
    gz_count = lax.axis_size("gz")
    gy_count = lax.axis_size("gy")
    gz = lax.axis_index("gz")
    gy = lax.axis_index("gy")
    bands_local, planes, columns = orbitals.shape
    n = points.shape[0]
    col_block = columns // gy_count
    half = col_block // 2
    slab = planes // gz_count
    pairs = gz_count // 2
    me = gz % 2
    total_bands = bands_local * gz_count * gy_count
    chunks = 2
    chunk = half // chunks

    def hop(array, bit):
        return lax.ppermute(array, "gz", [(z, z ^ bit) for z in range(gz_count)])

    def wait_for(array, other):
        return jnp.where(zero_after(other) == 0, array, jnp.zeros_like(array))

    def relay(both, other):
        first, second = both
        first = wait_for(first[:, rows // 2 :], other)
        second = wait_for(second[:, : rows // 2], other)
        return hop(second, 2), hop(first, 4)

    def gy_shift(array, by):
        return lax.ppermute(array, "gy", [(y, (y + by) % gy_count) for y in range(gy_count)])

    turned = jnp.transpose(orbitals, (2, 0, 1))
    blocks = turned.reshape(gy_count, 2, half, bands_local, planes)
    own = lax.dynamic_index_in_dim(blocks, me, 1, keepdims=False)
    partner = hop(lax.dynamic_index_in_dim(blocks, 1 - me, 1, keepdims=False), 1)

    values = take_points(points, turned.astype(F32), columns).astype(BF16)
    values = jnp.concatenate([values, hop(values, 1)], axis=0)
    values = jnp.concatenate(
        [values] + [gy_shift(values, dg) for dg in range(1, gy_count)], axis=0
    )
    column_values = values
    values = jnp.concatenate(
        [values] + [hop(values, 2 * p) for p in range(1, pairs)], axis=0
    )
    zero = zero_after(column_values[-1:])

    merged = jnp.concatenate([own, partner], axis=2)
    arriving = []
    for c in range(chunks):
        arriving.append([])
        for dg in range(gy_count):
            part = lax.dynamic_slice(
                merged,
                ((gy + dg + zero) % gy_count, c * chunk, 0, 0),
                (1, chunk, 2 * bands_local, planes),
            )[0]
            arriving[c].append(gy_shift(part, dg) if dg else part)

    steps = n // 256
    gram = sweep_gram(values, None, 0, ())

    fields = [None] * chunks
    rows = total_bands // pairs
    pending = None
    for step in range(1, steps):
        after = ()
        if step <= chunks:
            c = step - 1
            mine = wait_for(jnp.concatenate(arriving[c], axis=1), gram)
            after = (mine,)
            if pairs == 4:
                if pending is not None:
                    after = after + pending
                    fields[c - 1] = fields[c - 1] + relay(pending, gram)
                pending = (hop(mine, 2), hop(mine, 4))
                fields[c] = (mine,) + pending
            else:
                fields[c] = (mine,) + tuple(hop(mine, 2 * p) for p in range(1, pairs))
        elif pending is not None:
            after = pending
            fields[chunks - 1] = fields[chunks - 1] + relay(pending, gram)
            pending = None
        gram = sweep_gram(values, gram, step, after)
    inverse = gram

    grid = np.arange(planes, dtype=np.int64)
    table = np.cos((2.0 * np.pi / planes) * ((grid[:, None] * grid[None, :]) % planes))
    kernel = lax.dynamic_slice_in_dim(coulomb, me * half, half, 1).T
    lags = jnp.dot(
        kernel, jnp.asarray(table / planes, F32), precision=HIGH, preferred_element_type=F32
    )
    lags = jnp.stack([jnp.roll(lags, z * slab, axis=1) for z in (gz, gz ^ 1)])

    weights = ()
    for c in range(chunks):
        after = (inverse,) if c else ()
        weights = convolve(fields[c], values, lags, slab, c * chunk, weights, after)
    own_weights, other_weights = weights
    other_weights = hop(other_weights, 1)
    blocks_of_16 = half // 16
    result = fit((me * blocks_of_16)[None], own_weights, inverse, col_block, ())
    return fit(((1 - me) * blocks_of_16)[None], other_weights, inverse, col_block, (result,))


def solution(mesh):
    return jax.shard_map(
        per_device,
        mesh=mesh,
        in_specs=(P(("gz", "gy"), None, None), P(), P(None, "gy")),
        out_specs=P("gz", "gy", None),
        check_vma=False,
    )
```

```python
import functools
import math

import jax
import jax.numpy as jnp
import numpy as np
from jax import lax
from jax.experimental import pallas as pl
from jax.experimental.pallas import tpu as pltpu
from jax.sharding import PartitionSpec as P

F32 = jnp.float32
BF16 = jnp.bfloat16
HIGH = lax.Precision.HIGHEST
MIB = 1024 * 1024


def split(value):
    high = value.astype(BF16)
    return high, (value - high.astype(F32)).astype(BF16)


def points_kernel(where_ref, field_ref, out_ref):
    bands = field_ref.shape[1]
    lane = lax.broadcasted_iota(jnp.int32, (bands, 128), 1)

    def tile(t, _):
        base = pl.multiple_of(t * 128, 128)

        def some(s, accs):
            accs = list(accs)
            first = s * 32
            late = lane - first
            for u in range(32):
                m = first + u
                column = where_ref[0, base + m]
                at = pl.multiple_of(where_ref[1, base + m], 128)
                row = field_ref[column, :, pl.ds(at, 128)]
                row = pltpu.roll(row, where_ref[2, base + m], 1)
                accs[u % 4] = jnp.where(late == u, row, accs[u % 4])
            return tuple(accs)

        accs = lax.fori_loop(0, 4, some, (jnp.zeros((bands, 128), F32),) * 4)
        out_ref[:, pl.ds(base, 128)] = (accs[0] + accs[1]) + (accs[2] + accs[3])
        return 0

    lax.fori_loop(0, out_ref.shape[1] // 128, tile, 0)


def take_points(points, field, columns):
    plane = points // columns
    at = plane // 128 * 128
    shift = (jnp.arange(points.shape[0], dtype=jnp.int32) - plane) % 128
    where = jnp.stack([points - plane * columns, at, shift])
    return pl.pallas_call(
        points_kernel,
        out_shape=jax.ShapeDtypeStruct((field.shape[1], points.shape[0]), F32),
        in_specs=[
            pl.BlockSpec(memory_space=pltpu.SMEM),
            pl.BlockSpec(memory_space=pltpu.VMEM),
        ],
        out_specs=pl.BlockSpec(memory_space=pltpu.VMEM),
        compiler_params=pltpu.CompilerParams(vmem_limit_bytes=32 * MIB),
        name="take_points",
    )(where, field)


def total(terms):
    while len(terms) > 1:
        terms = [x + y for x, y in zip(terms[::2], terms[1::2])]
    return terms[0]


def sweep_small(a):
    n = a.shape[0]
    lane = lax.broadcasted_iota(jnp.int32, (8, n), 1)
    wide = lax.broadcasted_iota(jnp.int32, (n, n), 1)
    sub = lax.broadcasted_iota(jnp.int32, (8, n), 0)

    def spread(x, row):
        return jnp.broadcast_to(x[row : row + 1, :], (8, n))

    for g in range(n // 8):
        lo = 8 * g
        to = lo + 8
        rows = a[lo:to, :]
        cols = [jnp.broadcast_to(a[:, lo + j : lo + j + 1], (n, n)) for j in range(8)]
        t = {(i, j): spread(cols[j][lo:to, :], i) for i in range(8) for j in range(i + 1)}

        def at(i, j):
            return t[max(i, j), min(i, j)]

        for k in range(8):
            scale = 1.0 / t[k, k]
            old = {i: at(i, k) for i in range(8) if i != k}
            scaled = {i: old[i] * scale for i in old}
            for i in old:
                for j in old:
                    if j <= i:
                        t[i, j] = t[i, j] - scaled[i] * old[j]
                t[max(i, k), min(i, k)] = scaled[i]
            t[k, k] = -scale
        swept = []
        for j in range(8):
            column = at(0, j)
            for i in range(1, 8):
                column = jnp.where(sub == i, at(i, j), column)
            swept.append(column)
        q = -total([swept[j] * spread(rows, j) for j in range(8)])
        for j in range(8):
            q = jnp.where(lane == lo + j, swept[j], q)
        inside = (wide >= lo) & (wide < to)
        upd = jnp.where(inside, 0.0, a) - total(
            [cols[j] * jnp.broadcast_to(q[j : j + 1, :], (n, n)) for j in range(8)]
        )
        a = jnp.concatenate(([upd[:lo]] if lo else []) + [q] + ([upd[to:]] if to < n else []), axis=0)
    return a


def mm(a, b):
    return jnp.dot(a, b, precision=HIGH, preferred_element_type=F32)


def sweep_step(gram, block, panel, k, *, big, small):
    n = gram.shape[0]
    inner = lax.broadcasted_iota(jnp.int32, (small, big), 1)
    inner_full = lax.broadcasted_iota(jnp.int32, (big, big), 1)
    at = k * big
    kr = slice(at, at + big)
    block[...] = gram[kr, kr]
    for s in range(big // small):
        lo = s * small
        sr = slice(lo, lo + small)
        negative = sweep_small(block[sr, sr])
        q = -mm(negative, block[sr, :])
        inside = (inner >= lo) & (inner < lo + small)
        q = jnp.where(inside, jnp.concatenate([negative] * (big // small), axis=1), q)
        inside_full = (inner_full >= lo) & (inner_full < lo + small)
        upd = jnp.where(inside_full, 0.0, block[...]) - mm(block[:, sr], q)
        block[...] = upd
        block[sr, :] = q
    panel[...] = -mm(block[...], gram[kr, :])
    panel[:, kr] = block[...]
    wide = lax.broadcasted_iota(jnp.int32, (big, n), 1)
    inside = (wide >= at) & (wide < at + big)

    @pl.loop(0, n // big)
    def _(t):
        r = pl.ds(pl.multiple_of(t * big, big), big)
        col = gram[r, kr]
        gram[r, :] = jnp.where(inside, 0.0, gram[r, :]) - mm(col, panel[...])

    gram[kr, :] = panel[...]


def first_kernel(values_ref, gram, block, panel, *, big, small):
    @pl.loop(0, gram.shape[0] // big)
    def _(t):
        r = pl.ds(pl.multiple_of(t * big, big), big)
        base = lax.dot_general(
            values_ref[:, r], values_ref[...], (((0,), (0,)), ((), ())), preferred_element_type=F32
        )
        gram[r, :] = base * base

    sweep_step(gram, block, panel, 0, big=big, small=small)


def middle_kernel(*refs, step, big, small):
    gram, block, panel = refs[-3:]
    sweep_step(gram, block, panel, step, big=big, small=small)


def last_kernel(gram_ref, *refs, step, big, small):
    out_ref, gram, block, panel = refs[-4:]
    n = gram.shape[0]
    gram[...] = gram_ref[...]
    sweep_step(gram, block, panel, step, big=big, small=small)

    @pl.loop(0, n // big)
    def _(t):
        at = pl.multiple_of(t * big, big)
        high, low = split(-gram[pl.ds(at, big), :])
        out_ref[pl.ds(at, big), :] = high
        out_ref[pl.ds(at + n, big), :] = low


def sweep_gram(values, gram, step, after):
    big, small = 256, 128
    n = values.shape[1]
    last = step == n // big - 1
    vmem = pl.BlockSpec(memory_space=pltpu.VMEM)
    anywhere = pl.BlockSpec(memory_space=pl.ANY)
    state = jax.ShapeDtypeStruct((n, n), F32)
    scratch = [pltpu.VMEM((big, big), F32), pltpu.VMEM((big, n), F32)]
    options = dict(big=big, small=small)
    params = pltpu.CompilerParams(vmem_limit_bytes=16 * MIB)
    cost = pl.CostEstimate(flops=n * n, bytes_accessed=n * n, transcendentals=0)
    if step == 0:
        return pl.pallas_call(
            functools.partial(first_kernel, **options),
            out_shape=state,
            in_specs=[vmem],
            out_specs=vmem,
            scratch_shapes=scratch,
            compiler_params=params,
            cost_estimate=cost,
            name="sweep_first",
        )(values)
    specs = [vmem] + [anywhere] * len(after)
    if not last:
        return pl.pallas_call(
            functools.partial(middle_kernel, step=step, **options),
            out_shape=state,
            in_specs=specs,
            out_specs=vmem,
            scratch_shapes=scratch,
            input_output_aliases={0: 0},
            compiler_params=params,
            cost_estimate=cost,
            name="sweep_middle",
        )(gram, *after)
    return pl.pallas_call(
        functools.partial(last_kernel, step=step, **options),
        out_shape=jax.ShapeDtypeStruct((2 * n, n), BF16),
        in_specs=specs,
        out_specs=vmem,
        scratch_shapes=[pltpu.VMEM((n, n), F32)] + scratch,
        compiler_params=params,
        cost_estimate=cost,
        name="sweep_last",
    )(gram, *after)


def column_kernel(*refs, pieces, step):
    fields = refs[:pieces]
    values_ref, lags_ref, own_ref, other_ref = refs[pieces], refs[pieces + 1], refs[-2], refs[-1]
    tiles = own_ref.shape[0]
    slab = own_ref.shape[2] // 16
    planes = lags_ref.shape[2]
    inner = pl.program_id(1) * step
    first = pl.program_id(0) * 16 + inner
    turned = [jnp.concatenate([f[i] for f in fields], axis=0).T for i in range(step)]
    sums = jnp.dot(
        jnp.concatenate(turned, axis=0), values_ref[...], preferred_element_type=F32
    )
    for i in range(step):
        mine = sums[i * planes : (i + 1) * planes]
        high, low = split(mine * mine)
        circ = []
        for whose in range(2):
            row = jnp.broadcast_to(lags_ref[whose, pl.ds(first + i, 1), :], (slab, planes))
            circ.append(pltpu.roll(row, 0, 1, stride=1, stride_axis=0))
        circ = jnp.concatenate(split(jnp.concatenate(circ, axis=0)), axis=0)
        both = jnp.dot(
            jnp.concatenate([circ, circ], axis=1),
            jnp.concatenate([high, low], axis=0),
            preferred_element_type=F32,
        )
        w = both[: 2 * slab] + both[2 * slab :]
        rows = pl.ds(inner + i, slab, stride=16)
        for t in range(tiles):
            lanes = slice(t * 128, (t + 1) * 128)
            own_ref[t, 0, rows, :] = w[:slab, lanes]
            other_ref[t, 0, rows, :] = w[slab:, lanes]


def convolve(pieces, values, lags, slab, start, state, after):
    cols, _, planes = pieces[0].shape
    all_cols = lags.shape[1]
    bands, n = values.shape
    step = 4
    inner = 16 // step
    tiles = n // 128
    shape = jax.ShapeDtypeStruct((tiles, all_cols // 16, slab * 16, 128), F32)
    out_spec = pl.BlockSpec((tiles, 1, slab * 16, 128), lambda j, i: (0, j + start // 16, 0, 0))
    return pl.pallas_call(
        functools.partial(column_kernel, pieces=len(pieces), step=step),
        grid=(cols // 16, inner),
        out_shape=(shape, shape),
        in_specs=[
            pl.BlockSpec((step, p.shape[1], planes), lambda j, i: (j * inner + i, 0, 0))
            for p in pieces
        ]
        + [
            pl.BlockSpec((bands, n), lambda j, i: (0, 0)),
            pl.BlockSpec((2, cols, planes), lambda j, i: (0, start // cols, 0)),
        ]
        + [pl.BlockSpec(memory_space=pl.ANY)] * (len(state) + len(after)),
        out_specs=(out_spec, out_spec),
        input_output_aliases={len(pieces) + 2 + i: i for i in range(len(state))},
        compiler_params=pltpu.CompilerParams(vmem_limit_bytes=48 * MIB),
        cost_estimate=pl.CostEstimate(
            flops=2 * cols * n * planes * (bands + 8 * slab),
            bytes_accessed=2 * cols * (bands * planes + 4 * slab * n),
            transcendentals=0,
        ),
        name="convolve",
    )(*pieces, values, lags, *state, *after)


def fit_kernel(at_ref, w_ref, inverse_ref, *refs):
    out_ref = refs[-1]
    slab, cols, n = out_ref.shape
    w_high, w_low = split(jnp.concatenate([w_ref[t, 0] for t in range(n // 128)], axis=1))
    tile = 256
    for first in range(0, n, tile):
        lanes = slice(first, first + tile)
        high = inverse_ref[:n, lanes]
        out = jnp.dot(w_high, high, preferred_element_type=F32)
        out = out + jnp.dot(w_high, inverse_ref[n:, lanes], preferred_element_type=F32)
        out = out + jnp.dot(w_low, high, preferred_element_type=F32)
        out_ref[:, :, lanes] = out.reshape(slab, cols, tile).astype(out_ref.dtype)


def fit(at, w, inverse, width, state):
    tiles, blocks, rows, _ = w.shape
    n = tiles * 128
    step = 16
    slab = rows // step
    return pl.pallas_call(
        fit_kernel,
        grid_spec=pltpu.PrefetchScalarGridSpec(
            num_scalar_prefetch=1,
            grid=(blocks,),
            in_specs=[
                pl.BlockSpec((tiles, 1, rows, 128), lambda j, at: (0, j, 0, 0)),
                pl.BlockSpec((2 * n, n), lambda j, at: (0, 0)),
            ]
            + [pl.BlockSpec(memory_space=pl.ANY)] * len(state),
            out_specs=pl.BlockSpec((slab, step, n), lambda j, at: (0, j + at[0], 0)),
        ),
        out_shape=jax.ShapeDtypeStruct((slab, width, n), BF16),
        input_output_aliases={3: 0} if state else {},
        compiler_params=pltpu.CompilerParams(vmem_limit_bytes=56 * MIB),
        cost_estimate=pl.CostEstimate(
            flops=6 * blocks * rows * n * n,
            bytes_accessed=6 * blocks * rows * n + 4 * n * n,
            transcendentals=0,
        ),
        name="fit",
    )(at, w, inverse, *state)


def zero_after(array):
    return jnp.isnan(array[(0,) * array.ndim]).astype(jnp.int32)


def per_device(orbitals, points, coulomb):
    gz_count = lax.axis_size("gz")
    gy_count = lax.axis_size("gy")
    gz = lax.axis_index("gz")
    gy = lax.axis_index("gy")
    bands_local, planes, columns = orbitals.shape
    n = points.shape[0]
    col_block = columns // gy_count
    half = col_block // 2
    slab = planes // gz_count
    pairs = gz_count // 2
    me = gz % 2
    total_bands = bands_local * gz_count * gy_count
    chunks = 2
    chunk = half // chunks

    def hop(array, bit):
        return lax.ppermute(array, "gz", [(z, z ^ bit) for z in range(gz_count)])

    def wait_for(array, other):
        return jnp.where(zero_after(other) == 0, array, jnp.zeros_like(array))

    def relay(both, other):
        first, second = both
        first = wait_for(first[:, rows // 2 :], other)
        second = wait_for(second[:, : rows // 2], other)
        return hop(second, 2), hop(first, 4)

    def gy_shift(array, by):
        return lax.ppermute(array, "gy", [(y, (y + by) % gy_count) for y in range(gy_count)])

    turned = jnp.transpose(orbitals, (2, 0, 1))
    blocks = turned.reshape(gy_count, 2, half, bands_local, planes)
    own = lax.dynamic_index_in_dim(blocks, me, 1, keepdims=False)
    partner = hop(lax.dynamic_index_in_dim(blocks, 1 - me, 1, keepdims=False), 1)

    values = take_points(points, turned.astype(F32), columns).astype(BF16)
    values = jnp.concatenate([values, hop(values, 1)], axis=0)
    values = jnp.concatenate(
        [values] + [gy_shift(values, dg) for dg in range(1, gy_count)], axis=0
    )
    column_values = values
    values = jnp.concatenate(
        [values] + [hop(values, 2 * p) for p in range(1, pairs)], axis=0
    )
    zero = zero_after(column_values[-1:])

    merged = jnp.concatenate([own, partner], axis=2)
    arriving = []
    for c in range(chunks):
        arriving.append([])
        for dg in range(gy_count):
            part = lax.dynamic_slice(
                merged,
                ((gy + dg + zero) % gy_count, c * chunk, 0, 0),
                (1, chunk, 2 * bands_local, planes),
            )[0]
            arriving[c].append(gy_shift(part, dg) if dg else part)

    steps = n // 256
    gram = sweep_gram(values, None, 0, ())

    fields = [None] * chunks
    rows = total_bands // pairs
    pending = None
    for step in range(1, steps):
        after = ()
        if step <= chunks:
            c = step - 1
            mine = wait_for(jnp.concatenate(arriving[c], axis=1), gram)
            after = (mine,)
            if pairs == 4:
                if pending is not None:
                    after = after + pending
                    fields[c - 1] = fields[c - 1] + relay(pending, gram)
                pending = (hop(mine, 2), hop(mine, 4))
                fields[c] = (mine,) + pending
            else:
                fields[c] = (mine,) + tuple(hop(mine, 2 * p) for p in range(1, pairs))
        elif pending is not None:
            after = pending
            fields[chunks - 1] = fields[chunks - 1] + relay(pending, gram)
            pending = None
        gram = sweep_gram(values, gram, step, after)
    inverse = gram

    grid = np.arange(planes, dtype=np.int64)
    table = np.cos((2.0 * np.pi / planes) * ((grid[:, None] * grid[None, :]) % planes))
    kernel = lax.dynamic_slice_in_dim(coulomb, me * half, half, 1).T
    lags = jnp.dot(
        kernel, jnp.asarray(table / planes, F32), precision=HIGH, preferred_element_type=F32
    )
    lags = jnp.stack([jnp.roll(lags, z * slab, axis=1) for z in (gz, gz ^ 1)])

    weights = ()
    for c in range(chunks):
        after = (inverse,) if c else ()
        weights = convolve(fields[c], values, lags, slab, c * chunk, weights, after)
    own_weights, other_weights = weights
    other_weights = hop(other_weights, 1)
    blocks_of_16 = half // 16
    result = fit((me * blocks_of_16)[None], own_weights, inverse, col_block, ())
    return fit(((1 - me) * blocks_of_16)[None], other_weights, inverse, col_block, (result,))


def solution(mesh):
    return jax.shard_map(
        per_device,
        mesh=mesh,
        in_specs=(P(("gz", "gy"), None, None), P(), P(None, "gy")),
        out_specs=P("gz", "gy", None),
        check_vma=False,
    )
```

```python
import functools
import math

import jax
import jax.numpy as jnp
import numpy as np
from jax import lax
from jax.experimental import pallas as pl
from jax.experimental.pallas import tpu as pltpu
from jax.sharding import PartitionSpec as P

F32 = jnp.float32
BF16 = jnp.bfloat16
HIGH = lax.Precision.HIGHEST
MIB = 1024 * 1024


def split(value):
    high = value.astype(BF16)
    return high, (value - high.astype(F32)).astype(BF16)


def points_kernel(where_ref, field_ref, out_ref):
    bands = field_ref.shape[1]
    lane = lax.broadcasted_iota(jnp.int32, (bands, 128), 1)

    def tile(t, _):
        base = pl.multiple_of(t * 128, 128)

        def some(s, accs):
            accs = list(accs)
            first = s * 32
            late = lane - first
            for u in range(32):
                m = first + u
                column = where_ref[0, base + m]
                at = pl.multiple_of(where_ref[1, base + m], 128)
                row = field_ref[column, :, pl.ds(at, 128)]
                row = pltpu.roll(row, where_ref[2, base + m], 1)
                accs[u % 4] = jnp.where(late == u, row, accs[u % 4])
            return tuple(accs)

        accs = lax.fori_loop(0, 4, some, (jnp.zeros((bands, 128), F32),) * 4)
        out_ref[:, pl.ds(base, 128)] = (accs[0] + accs[1]) + (accs[2] + accs[3])
        return 0

    lax.fori_loop(0, out_ref.shape[1] // 128, tile, 0)


def take_points(points, field, columns):
    plane = points // columns
    at = plane // 128 * 128
    shift = (jnp.arange(points.shape[0], dtype=jnp.int32) - plane) % 128
    where = jnp.stack([points - plane * columns, at, shift])
    return pl.pallas_call(
        points_kernel,
        out_shape=jax.ShapeDtypeStruct((field.shape[1], points.shape[0]), F32),
        in_specs=[
            pl.BlockSpec(memory_space=pltpu.SMEM),
            pl.BlockSpec(memory_space=pltpu.VMEM),
        ],
        out_specs=pl.BlockSpec(memory_space=pltpu.VMEM),
        compiler_params=pltpu.CompilerParams(vmem_limit_bytes=32 * MIB),
        name="take_points",
    )(where, field)


def sweep_small(a):
    n = a.shape[0]
    lane = lax.broadcasted_iota(jnp.int32, (8, n), 1)
    wide = lax.broadcasted_iota(jnp.int32, (n, n), 1)
    sub = lax.broadcasted_iota(jnp.int32, (8, n), 0)
    for g in range(n // 8):
        lo = 8 * g
        rows = a[lo : lo + 8, :]
        cols = [jnp.broadcast_to(a[:, lo + j : lo + j + 1], (n, n)) for j in range(8)]
        t = [c[lo : lo + 8, :] for c in cols]
        for k in range(8):
            pivot = jnp.broadcast_to(t[k][k : k + 1, :], (8, n))
            scale = 1.0 / pivot
            here = sub == k
            new = []
            for j in range(8):
                if j == k:
                    new.append(jnp.where(here, -1.0, t[k]) * scale)
                else:
                    factor = jnp.broadcast_to(t[j][k : k + 1, :], (8, n))
                    kept = jnp.where(here, 0.0, t[j])
                    new.append(kept - (jnp.where(here, -1.0, t[k]) * factor) * scale)
            t = new
        terms = [t[j] * jnp.broadcast_to(rows[j : j + 1, :], (8, n)) for j in range(8)]
        while len(terms) > 1:
            terms = [x + y for x, y in zip(terms[::2], terms[1::2])]
        q = -terms[0]
        for j in range(8):
            q = jnp.where(lane == lo + j, t[j], q)
        inside = (wide >= lo) & (wide < lo + 8)
        terms = [cols[j] * jnp.broadcast_to(q[j : j + 1, :], (n, n)) for j in range(8)]
        while len(terms) > 1:
            terms = [x + y for x, y in zip(terms[::2], terms[1::2])]
        upd = jnp.where(inside, 0.0, a) - terms[0]
        a = jnp.concatenate(
            ([upd[:lo]] if lo else []) + [q] + ([upd[lo + 8 :]] if lo + 8 < n else []), axis=0
        )
    return a


def mm(a, b):
    return jnp.dot(a, b, precision=HIGH, preferred_element_type=F32)


def sweep_step(gram, block, panel, k, *, big, small):
    n = gram.shape[0]
    inner = lax.broadcasted_iota(jnp.int32, (small, big), 1)
    inner_full = lax.broadcasted_iota(jnp.int32, (big, big), 1)
    at = k * big
    kr = slice(at, at + big)
    block[...] = gram[kr, kr]
    for s in range(big // small):
        lo = s * small
        sr = slice(lo, lo + small)
        negative = sweep_small(block[sr, sr])
        q = -mm(negative, block[sr, :])
        inside = (inner >= lo) & (inner < lo + small)
        q = jnp.where(inside, jnp.concatenate([negative] * (big // small), axis=1), q)
        inside_full = (inner_full >= lo) & (inner_full < lo + small)
        upd = jnp.where(inside_full, 0.0, block[...]) - mm(block[:, sr], q)
        block[...] = upd
        block[sr, :] = q
    panel[...] = -mm(block[...], gram[kr, :])
    panel[:, kr] = block[...]
    wide = lax.broadcasted_iota(jnp.int32, (big, n), 1)
    inside = (wide >= at) & (wide < at + big)

    @pl.loop(0, n // big)
    def _(t):
        r = pl.ds(pl.multiple_of(t * big, big), big)
        col = gram[r, kr]
        gram[r, :] = jnp.where(inside, 0.0, gram[r, :]) - mm(col, panel[...])

    gram[kr, :] = panel[...]


def first_kernel(values_ref, *refs, big, small):
    gram, block, panel = refs[-3:]

    @pl.loop(0, gram.shape[0] // big)
    def _(t):
        r = pl.ds(pl.multiple_of(t * big, big), big)
        base = lax.dot_general(
            values_ref[:, r], values_ref[...], (((0,), (0,)), ((), ())), preferred_element_type=F32
        )
        gram[r, :] = base * base

    sweep_step(gram, block, panel, 0, big=big, small=small)


def middle_kernel(*refs, step, big, small):
    gram, block, panel = refs[-3:]
    sweep_step(gram, block, panel, step, big=big, small=small)


def last_kernel(gram_ref, *refs, step, big, small):
    out_ref, gram, block, panel = refs[-4:]
    n = gram.shape[0]
    gram[...] = gram_ref[...]
    sweep_step(gram, block, panel, step, big=big, small=small)

    @pl.loop(0, n // big)
    def _(t):
        at = pl.multiple_of(t * big, big)
        high, low = split(-gram[pl.ds(at, big), :])
        out_ref[pl.ds(at, big), :] = high
        out_ref[pl.ds(at + n, big), :] = low


def sweep_gram(values, gram, step, after):
    big, small = 256, 128
    n = values.shape[1]
    last = step == n // big - 1
    vmem = pl.BlockSpec(memory_space=pltpu.VMEM)
    anywhere = pl.BlockSpec(memory_space=pl.ANY)
    state = jax.ShapeDtypeStruct((n, n), F32)
    scratch = [pltpu.VMEM((big, big), F32), pltpu.VMEM((big, n), F32)]
    options = dict(big=big, small=small)
    params = pltpu.CompilerParams(vmem_limit_bytes=16 * MIB)
    cost = pl.CostEstimate(flops=n * n, bytes_accessed=n * n, transcendentals=0)
    if step == 0:
        return pl.pallas_call(
            functools.partial(first_kernel, **options),
            out_shape=state,
            in_specs=[vmem] + [anywhere] * len(after),
            out_specs=vmem,
            scratch_shapes=scratch,
            compiler_params=params,
            cost_estimate=cost,
            name="sweep_first",
        )(values, *after)
    specs = [vmem] + [anywhere] * len(after)
    if not last:
        return pl.pallas_call(
            functools.partial(middle_kernel, step=step, **options),
            out_shape=state,
            in_specs=specs,
            out_specs=vmem,
            scratch_shapes=scratch,
            input_output_aliases={0: 0},
            compiler_params=params,
            cost_estimate=cost,
            name="sweep_middle",
        )(gram, *after)
    return pl.pallas_call(
        functools.partial(last_kernel, step=step, **options),
        out_shape=jax.ShapeDtypeStruct((2 * n, n), BF16),
        in_specs=specs,
        out_specs=vmem,
        scratch_shapes=[pltpu.VMEM((n, n), F32)] + scratch,
        compiler_params=params,
        cost_estimate=cost,
        name="sweep_last",
    )(gram, *after)


def column_kernel(*refs, pieces):
    fields = refs[:pieces]
    values_ref, lags_ref, own_ref, other_ref = refs[pieces], refs[pieces + 1], refs[-2], refs[-1]
    step, slab, _ = own_ref.shape
    n = values_ref.shape[1]
    planes = lags_ref.shape[2]
    first = pl.program_id(0) * step
    turned = [jnp.concatenate([f[i] for f in fields], axis=0).T for i in range(step)]
    sums = jnp.dot(
        jnp.concatenate(turned, axis=0), values_ref[...], preferred_element_type=F32
    )
    for i in range(step):
        mine = sums[i * planes : (i + 1) * planes]
        high, low = split(mine * mine)
        circ = []
        for whose in range(2):
            row = jnp.broadcast_to(lags_ref[whose, pl.ds(first + i, 1), :], (slab, planes))
            circ.append(pltpu.roll(row, 0, 1, stride=1, stride_axis=0))
        circ = jnp.concatenate(split(jnp.concatenate(circ, axis=0)), axis=0)
        both = jnp.dot(
            jnp.concatenate([circ, circ], axis=1),
            jnp.concatenate([high, low], axis=0),
            preferred_element_type=F32,
        )
        w_high, w_low = split(both[: 2 * slab] + both[2 * slab :])
        own_ref[i, :, :n] = w_high[:slab]
        own_ref[i, :, n:] = w_low[:slab]
        other_ref[i, :, :n] = w_high[slab:]
        other_ref[i, :, n:] = w_low[slab:]


def convolve(pieces, values, lags, slab, start, state, after):
    cols, _, planes = pieces[0].shape
    all_cols = lags.shape[1]
    bands, n = values.shape
    step = 4
    shape = jax.ShapeDtypeStruct((all_cols, slab, 2 * n), BF16)
    out_spec = pl.BlockSpec((step, slab, 2 * n), lambda j: (j + start // step, 0, 0))
    return pl.pallas_call(
        functools.partial(column_kernel, pieces=len(pieces)),
        grid=(cols // step,),
        out_shape=(shape, shape),
        in_specs=[pl.BlockSpec((step, p.shape[1], planes), lambda j: (j, 0, 0)) for p in pieces]
        + [
            pl.BlockSpec((bands, n), lambda j: (0, 0)),
            pl.BlockSpec((2, cols, planes), lambda j: (0, start // cols, 0)),
        ]
        + [pl.BlockSpec(memory_space=pl.ANY)] * (len(state) + len(after)),
        out_specs=(out_spec, out_spec),
        input_output_aliases={len(pieces) + 2 + i: i for i in range(len(state))},
        compiler_params=pltpu.CompilerParams(vmem_limit_bytes=48 * MIB),
        cost_estimate=pl.CostEstimate(
            flops=2 * cols * n * planes * (bands + 8 * slab),
            bytes_accessed=2 * cols * (bands * planes + 4 * slab * n),
            transcendentals=0,
        ),
        name="convolve",
    )(*pieces, values, lags, *state, *after)


def fit_kernel(at_ref, w_ref, inverse_ref, *refs):
    out_ref, turn = refs[-2:]
    slab, cols, n = out_ref.shape
    w = w_ref[...].reshape(cols * slab, 2 * n)
    w_high, w_low = w[:, :n], w[:, n:]
    tile = 256
    for first in range(0, n, tile):
        lanes = slice(first, first + tile)
        high = inverse_ref[:n, lanes]
        out = jnp.dot(w_high, high, preferred_element_type=F32)
        out = out + jnp.dot(w_high, inverse_ref[n:, lanes], preferred_element_type=F32)
        out = out + jnp.dot(w_low, high, preferred_element_type=F32)
        for t in range(tile // 128):
            at = first // 128 + t
            part = slice(t * 128, (t + 1) * 128)
            for c in range(cols):
                turn[at, pl.ds(c, slab, stride=cols), :] = out[c * slab : (c + 1) * slab, part]
            out_ref[:, :, at * 128 : (at + 1) * 128] = (
                turn[at].reshape(slab, cols, 128).astype(out_ref.dtype)
            )


def fit(at, w, inverse, width, state):
    cols, slab, n2 = w.shape
    n = n2 // 2
    step = 16
    return pl.pallas_call(
        fit_kernel,
        grid_spec=pltpu.PrefetchScalarGridSpec(
            num_scalar_prefetch=1,
            grid=(cols // step,),
            in_specs=[
                pl.BlockSpec((step, slab, n2), lambda j, at: (j, 0, 0)),
                pl.BlockSpec((2 * n, n), lambda j, at: (0, 0)),
            ]
            + [pl.BlockSpec(memory_space=pl.ANY)] * len(state),
            out_specs=pl.BlockSpec((slab, step, n), lambda j, at: (0, j + at[0], 0)),
            scratch_shapes=[pltpu.VMEM((n // 128, slab * step, 128), F32)],
        ),
        out_shape=jax.ShapeDtypeStruct((slab, width, n), BF16),
        input_output_aliases={3: 0} if state else {},
        compiler_params=pltpu.CompilerParams(vmem_limit_bytes=56 * MIB),
        cost_estimate=pl.CostEstimate(
            flops=6 * cols * slab * n * n,
            bytes_accessed=6 * cols * slab * n + 4 * n * n,
            transcendentals=0,
        ),
        name="fit",
    )(at, w, inverse, *state)


def zero_after(array):
    return jnp.isnan(array[(0,) * array.ndim]).astype(jnp.int32)


def per_device(orbitals, points, coulomb):
    gz_count = lax.axis_size("gz")
    gy_count = lax.axis_size("gy")
    gz = lax.axis_index("gz")
    gy = lax.axis_index("gy")
    bands_local, planes, columns = orbitals.shape
    n = points.shape[0]
    col_block = columns // gy_count
    half = col_block // 2
    slab = planes // gz_count
    pairs = gz_count // 2
    me = gz % 2
    total_bands = bands_local * gz_count * gy_count
    chunks = 2
    chunk = half // chunks

    def hop(array, bit):
        return lax.ppermute(array, "gz", [(z, z ^ bit) for z in range(gz_count)])

    def wait_for(array, other):
        return jnp.where(zero_after(other) == 0, array, jnp.zeros_like(array))

    def relay(both, other):
        first, second = both
        first = wait_for(first[:, rows // 2 :], other)
        second = wait_for(second[:, : rows // 2], other)
        return hop(second, 2), hop(first, 4)

    def gy_shift(array, by):
        return lax.ppermute(array, "gy", [(y, (y + by) % gy_count) for y in range(gy_count)])

    turned = jnp.transpose(orbitals, (2, 0, 1))
    blocks = turned.reshape(gy_count, 2, half, bands_local, planes)
    own = lax.dynamic_index_in_dim(blocks, me, 1, keepdims=False)
    partner = hop(lax.dynamic_index_in_dim(blocks, 1 - me, 1, keepdims=False), 1)

    values = take_points(points, turned.astype(F32), columns).astype(BF16)
    values = jnp.concatenate([values, hop(values, 1)], axis=0)
    values = jnp.concatenate(
        [values] + [gy_shift(values, dg) for dg in range(1, gy_count)], axis=0
    )
    column_values = values
    values = jnp.concatenate(
        [values] + [hop(values, 2 * p) for p in range(1, pairs)], axis=0
    )
    zero = zero_after(column_values[-1:])

    merged = jnp.concatenate([own, partner], axis=2)
    arriving = []
    for c in range(chunks):
        arriving.append([])
        for dg in range(gy_count):
            part = lax.dynamic_slice(
                merged,
                ((gy + dg + zero) % gy_count, c * chunk, 0, 0),
                (1, chunk, 2 * bands_local, planes),
            )[0]
            arriving[c].append(gy_shift(part, dg) if dg else part)

    grid = np.arange(planes, dtype=np.int64)
    table = np.cos((2.0 * np.pi / planes) * ((grid[:, None] * grid[None, :]) % planes))
    kernel = lax.dynamic_slice_in_dim(coulomb, me * half, half, 1).T
    lags = jnp.dot(
        kernel, jnp.asarray(table / planes, F32), precision=HIGH, preferred_element_type=F32
    )
    lags = jnp.stack([jnp.roll(lags, z * slab, axis=1) for z in (gz, gz ^ 1)])

    steps = n // 256
    gram = sweep_gram(values, None, 0, (lags,))

    fields = [None] * chunks
    rows = total_bands // pairs
    pending = None
    for step in range(1, steps):
        after = ()
        if step <= chunks:
            c = step - 1
            mine = wait_for(jnp.concatenate(arriving[c], axis=1), gram)
            after = (mine,)
            if pairs == 4:
                if pending is not None:
                    after = after + pending
                    fields[c - 1] = fields[c - 1] + relay(pending, gram)
                pending = (hop(mine, 2), hop(mine, 4))
                fields[c] = (mine,) + pending
            else:
                fields[c] = (mine,) + tuple(hop(mine, 2 * p) for p in range(1, pairs))
        elif pending is not None:
            after = pending
            fields[chunks - 1] = fields[chunks - 1] + relay(pending, gram)
            pending = None
        gram = sweep_gram(values, gram, step, after)
    inverse = gram

    weights = ()
    for c in range(chunks):
        after = (inverse,) if c else ()
        weights = convolve(fields[c], values, lags, slab, c * chunk, weights, after)
    own_weights, other_weights = weights
    other_weights = hop(other_weights, 1)
    blocks_of_16 = half // 16
    result = fit((me * blocks_of_16)[None], own_weights, inverse, col_block, ())
    return fit(((1 - me) * blocks_of_16)[None], other_weights, inverse, col_block, (result,))


def solution(mesh):
    return jax.shard_map(
        per_device,
        mesh=mesh,
        in_specs=(P(("gz", "gy"), None, None), P(), P(None, "gy")),
        out_specs=P("gz", "gy", None),
        check_vma=False,
    )
```

```python
import functools
import math

import jax
import jax.numpy as jnp
import numpy as np
from jax import lax
from jax.experimental import pallas as pl
from jax.experimental.pallas import tpu as pltpu
from jax.sharding import PartitionSpec as P

F32 = jnp.float32
BF16 = jnp.bfloat16
HIGH = lax.Precision.HIGHEST
MIB = 1024 * 1024


def split(value):
    high = value.astype(BF16)
    return high, (value - high.astype(F32)).astype(BF16)


def points_kernel(where_ref, field_ref, out_ref):
    bands = field_ref.shape[1]
    lane = lax.broadcasted_iota(jnp.int32, (bands, 128), 1)

    def tile(t, _):
        base = pl.multiple_of(t * 128, 128)

        def some(s, accs):
            accs = list(accs)
            first = s * 32
            late = lane - first
            for u in range(32):
                m = first + u
                column = where_ref[0, base + m]
                at = pl.multiple_of(where_ref[1, base + m], 128)
                row = field_ref[column, :, pl.ds(at, 128)]
                row = pltpu.roll(row, where_ref[2, base + m], 1)
                accs[u % 4] = jnp.where(late == u, row, accs[u % 4])
            return tuple(accs)

        accs = lax.fori_loop(0, 4, some, (jnp.zeros((bands, 128), F32),) * 4)
        out_ref[:, pl.ds(base, 128)] = (accs[0] + accs[1]) + (accs[2] + accs[3])
        return 0

    lax.fori_loop(0, out_ref.shape[1] // 128, tile, 0)


def take_points(points, field, columns):
    plane = points // columns
    at = plane // 128 * 128
    shift = (jnp.arange(points.shape[0], dtype=jnp.int32) - plane) % 128
    where = jnp.stack([points - plane * columns, at, shift])
    return pl.pallas_call(
        points_kernel,
        out_shape=jax.ShapeDtypeStruct((field.shape[1], points.shape[0]), F32),
        in_specs=[
            pl.BlockSpec(memory_space=pltpu.SMEM),
            pl.BlockSpec(memory_space=pltpu.VMEM),
        ],
        out_specs=pl.BlockSpec(memory_space=pltpu.VMEM),
        compiler_params=pltpu.CompilerParams(vmem_limit_bytes=32 * MIB),
        name="take_points",
    )(where, field)


def total(terms):
    while len(terms) > 1:
        terms = [x + y for x, y in zip(terms[::2], terms[1::2])]
    return terms[0]


def sweep_small(a):
    n = a.shape[0]
    lane = lax.broadcasted_iota(jnp.int32, (8, n), 1)
    sub = lax.broadcasted_iota(jnp.int32, (8, n), 0)
    tiles = [a[i : i + 8, :] for i in range(0, n, 8)]

    def spread_row(x, row):
        return jnp.broadcast_to(x[row : row + 1, :], (8, n))

    def spread_column(x, column):
        return jnp.broadcast_to(x[:, column : column + 1], (8, n))

    for g in range(n // 8):
        lo = 8 * g
        rows = tiles[g]
        t = [spread_column(rows, lo + j) for j in range(8)]
        for k in range(8):
            here = sub == k
            pivot = jnp.where(here, -1.0, t[k]) * (1.0 / spread_row(t[k], k))
            t = [
                pivot if j == k else jnp.where(here, 0.0, t[j]) - pivot * spread_row(t[j], k)
                for j in range(8)
            ]
        q = -total([t[j] * spread_row(rows, j) for j in range(8)])
        for j in range(8):
            q = jnp.where(lane == lo + j, t[j], q)
        inside = (lane >= lo) & (lane < lo + 8)
        q_rows = [spread_row(q, j) for j in range(8)]
        tiles = [
            q
            if i == g
            else jnp.where(inside, 0.0, tile)
            - total([spread_column(tile, lo + j) * q_rows[j] for j in range(8)])
            for i, tile in enumerate(tiles)
        ]
    return jnp.concatenate(tiles, axis=0)


def mm(a, b):
    return jnp.dot(a, b, precision=HIGH, preferred_element_type=F32)


def sweep_step(gram, block, panel, k, *, big, small):
    n = gram.shape[0]
    inner = lax.broadcasted_iota(jnp.int32, (small, big), 1)
    inner_full = lax.broadcasted_iota(jnp.int32, (big, big), 1)
    at = k * big
    kr = slice(at, at + big)
    block[...] = gram[kr, kr]
    for s in range(big // small):
        lo = s * small
        sr = slice(lo, lo + small)
        negative = sweep_small(block[sr, sr])
        q = -mm(negative, block[sr, :])
        inside = (inner >= lo) & (inner < lo + small)
        q = jnp.where(inside, jnp.concatenate([negative] * (big // small), axis=1), q)
        inside_full = (inner_full >= lo) & (inner_full < lo + small)
        upd = jnp.where(inside_full, 0.0, block[...]) - mm(block[:, sr], q)
        block[...] = upd
        block[sr, :] = q
    panel[...] = -mm(block[...], gram[kr, :])
    panel[:, kr] = block[...]
    wide = lax.broadcasted_iota(jnp.int32, (big, n), 1)
    inside = (wide >= at) & (wide < at + big)

    @pl.loop(0, n // big)
    def _(t):
        r = pl.ds(pl.multiple_of(t * big, big), big)
        col = gram[r, kr]
        gram[r, :] = jnp.where(inside, 0.0, gram[r, :]) - mm(col, panel[...])

    gram[kr, :] = panel[...]


def first_kernel(values_ref, *refs, big, small):
    gram, block, panel = refs[-3:]

    @pl.loop(0, gram.shape[0] // big)
    def _(t):
        r = pl.ds(pl.multiple_of(t * big, big), big)
        base = lax.dot_general(
            values_ref[:, r], values_ref[...], (((0,), (0,)), ((), ())), preferred_element_type=F32
        )
        gram[r, :] = base * base

    sweep_step(gram, block, panel, 0, big=big, small=small)


def middle_kernel(*refs, step, big, small):
    gram, block, panel = refs[-3:]
    sweep_step(gram, block, panel, step, big=big, small=small)


def last_kernel(gram_ref, *refs, step, big, small):
    out_ref, gram, block, panel = refs[-4:]
    n = gram.shape[0]
    gram[...] = gram_ref[...]
    sweep_step(gram, block, panel, step, big=big, small=small)

    @pl.loop(0, n // big)
    def _(t):
        at = pl.multiple_of(t * big, big)
        high, low = split(-gram[pl.ds(at, big), :])
        out_ref[pl.ds(at, big), :] = high
        out_ref[pl.ds(at + n, big), :] = low


def sweep_gram(values, gram, step, after):
    big, small = 256, 128
    n = values.shape[1]
    last = step == n // big - 1
    vmem = pl.BlockSpec(memory_space=pltpu.VMEM)
    anywhere = pl.BlockSpec(memory_space=pl.ANY)
    state = jax.ShapeDtypeStruct((n, n), F32)
    scratch = [pltpu.VMEM((big, big), F32), pltpu.VMEM((big, n), F32)]
    options = dict(big=big, small=small)
    params = pltpu.CompilerParams(vmem_limit_bytes=16 * MIB)
    cost = pl.CostEstimate(flops=n * n, bytes_accessed=n * n, transcendentals=0)
    if step == 0:
        return pl.pallas_call(
            functools.partial(first_kernel, **options),
            out_shape=state,
            in_specs=[vmem] + [anywhere] * len(after),
            out_specs=vmem,
            scratch_shapes=scratch,
            compiler_params=params,
            cost_estimate=cost,
            name="sweep_first",
        )(values, *after)
    specs = [vmem] + [anywhere] * len(after)
    if not last:
        return pl.pallas_call(
            functools.partial(middle_kernel, step=step, **options),
            out_shape=state,
            in_specs=specs,
            out_specs=vmem,
            scratch_shapes=scratch,
            input_output_aliases={0: 0},
            compiler_params=params,
            cost_estimate=cost,
            name="sweep_middle",
        )(gram, *after)
    return pl.pallas_call(
        functools.partial(last_kernel, step=step, **options),
        out_shape=jax.ShapeDtypeStruct((2 * n, n), BF16),
        in_specs=specs,
        out_specs=vmem,
        scratch_shapes=[pltpu.VMEM((n, n), F32)] + scratch,
        compiler_params=params,
        cost_estimate=cost,
        name="sweep_last",
    )(gram, *after)


def column_kernel(*refs, pieces):
    fields = refs[:pieces]
    values_ref, lags_ref, own_ref, other_ref = refs[pieces], refs[pieces + 1], refs[-2], refs[-1]
    step, slab, _ = own_ref.shape
    n = values_ref.shape[1]
    planes = lags_ref.shape[2]
    first = pl.program_id(0) * step
    turned = [jnp.concatenate([f[i] for f in fields], axis=0).T for i in range(step)]
    sums = jnp.dot(
        jnp.concatenate(turned, axis=0), values_ref[...], preferred_element_type=F32
    )
    for i in range(step):
        mine = sums[i * planes : (i + 1) * planes]
        high, low = split(mine * mine)
        circ = []
        for whose in range(2):
            row = jnp.broadcast_to(lags_ref[whose, pl.ds(first + i, 1), :], (slab, planes))
            circ.append(pltpu.roll(row, 0, 1, stride=1, stride_axis=0))
        circ = jnp.concatenate(split(jnp.concatenate(circ, axis=0)), axis=0)
        both = jnp.dot(
            jnp.concatenate([circ, circ], axis=1),
            jnp.concatenate([high, low], axis=0),
            preferred_element_type=F32,
        )
        w_high, w_low = split(both[: 2 * slab] + both[2 * slab :])
        own_ref[i, :, :n] = w_high[:slab]
        own_ref[i, :, n:] = w_low[:slab]
        other_ref[i, :, :n] = w_high[slab:]
        other_ref[i, :, n:] = w_low[slab:]


def convolve(pieces, values, lags, slab, start, state, after):
    cols, _, planes = pieces[0].shape
    all_cols = lags.shape[1]
    bands, n = values.shape
    step = 4
    shape = jax.ShapeDtypeStruct((all_cols, slab, 2 * n), BF16)
    out_spec = pl.BlockSpec((step, slab, 2 * n), lambda j: (j + start // step, 0, 0))
    return pl.pallas_call(
        functools.partial(column_kernel, pieces=len(pieces)),
        grid=(cols // step,),
        out_shape=(shape, shape),
        in_specs=[pl.BlockSpec((step, p.shape[1], planes), lambda j: (j, 0, 0)) for p in pieces]
        + [
            pl.BlockSpec((bands, n), lambda j: (0, 0)),
            pl.BlockSpec((2, cols, planes), lambda j: (0, start // cols, 0)),
        ]
        + [pl.BlockSpec(memory_space=pl.ANY)] * (len(state) + len(after)),
        out_specs=(out_spec, out_spec),
        input_output_aliases={len(pieces) + 2 + i: i for i in range(len(state))},
        compiler_params=pltpu.CompilerParams(vmem_limit_bytes=48 * MIB),
        cost_estimate=pl.CostEstimate(
            flops=2 * cols * n * planes * (bands + 8 * slab),
            bytes_accessed=2 * cols * (bands * planes + 4 * slab * n),
            transcendentals=0,
        ),
        name="convolve",
    )(*pieces, values, lags, *state, *after)


def fit_kernel(at_ref, w_ref, inverse_ref, *refs):
    out_ref, turn = refs[-2:]
    slab, cols, n = out_ref.shape
    w = w_ref[...].reshape(cols * slab, 2 * n)
    w_high, w_low = w[:, :n], w[:, n:]
    tile = 256
    for first in range(0, n, tile):
        lanes = slice(first, first + tile)
        high = inverse_ref[:n, lanes]
        out = jnp.dot(w_high, high, preferred_element_type=F32)
        out = out + jnp.dot(w_high, inverse_ref[n:, lanes], preferred_element_type=F32)
        out = out + jnp.dot(w_low, high, preferred_element_type=F32)
        for t in range(tile // 128):
            at = first // 128 + t
            part = slice(t * 128, (t + 1) * 128)
            for c in range(cols):
                turn[at, pl.ds(c, slab, stride=cols), :] = out[c * slab : (c + 1) * slab, part]
            out_ref[:, :, at * 128 : (at + 1) * 128] = (
                turn[at].reshape(slab, cols, 128).astype(out_ref.dtype)
            )


def fit(at, w, inverse, width, state):
    cols, slab, n2 = w.shape
    n = n2 // 2
    step = 16
    return pl.pallas_call(
        fit_kernel,
        grid_spec=pltpu.PrefetchScalarGridSpec(
            num_scalar_prefetch=1,
            grid=(cols // step,),
            in_specs=[
                pl.BlockSpec((step, slab, n2), lambda j, at: (j, 0, 0)),
                pl.BlockSpec((2 * n, n), lambda j, at: (0, 0)),
            ]
            + [pl.BlockSpec(memory_space=pl.ANY)] * len(state),
            out_specs=pl.BlockSpec((slab, step, n), lambda j, at: (0, j + at[0], 0)),
            scratch_shapes=[pltpu.VMEM((n // 128, slab * step, 128), F32)],
        ),
        out_shape=jax.ShapeDtypeStruct((slab, width, n), BF16),
        input_output_aliases={3: 0} if state else {},
        compiler_params=pltpu.CompilerParams(vmem_limit_bytes=56 * MIB),
        cost_estimate=pl.CostEstimate(
            flops=6 * cols * slab * n * n,
            bytes_accessed=6 * cols * slab * n + 4 * n * n,
            transcendentals=0,
        ),
        name="fit",
    )(at, w, inverse, *state)


def zero_after(array):
    return jnp.isnan(array[(0,) * array.ndim]).astype(jnp.int32)


def per_device(orbitals, points, coulomb):
    gz_count = lax.axis_size("gz")
    gy_count = lax.axis_size("gy")
    gz = lax.axis_index("gz")
    gy = lax.axis_index("gy")
    bands_local, planes, columns = orbitals.shape
    n = points.shape[0]
    col_block = columns // gy_count
    half = col_block // 2
    slab = planes // gz_count
    pairs = gz_count // 2
    me = gz % 2
    total_bands = bands_local * gz_count * gy_count
    chunks = 2
    chunk = half // chunks

    def hop(array, bit):
        return lax.ppermute(array, "gz", [(z, z ^ bit) for z in range(gz_count)])

    def wait_for(array, other):
        return jnp.where(zero_after(other) == 0, array, jnp.zeros_like(array))

    def relay(both, other):
        first, second = both
        first = wait_for(first[:, rows // 2 :], other)
        second = wait_for(second[:, : rows // 2], other)
        return hop(second, 2), hop(first, 4)

    def gy_shift(array, by):
        return lax.ppermute(array, "gy", [(y, (y + by) % gy_count) for y in range(gy_count)])

    turned = jnp.transpose(orbitals, (2, 0, 1))
    blocks = turned.reshape(gy_count, 2, half, bands_local, planes)
    own = lax.dynamic_index_in_dim(blocks, me, 1, keepdims=False)
    partner = hop(lax.dynamic_index_in_dim(blocks, 1 - me, 1, keepdims=False), 1)

    values = take_points(points, turned.astype(F32), columns).astype(BF16)
    values = jnp.concatenate([values, hop(values, 1)], axis=0)
    values = jnp.concatenate(
        [values] + [gy_shift(values, dg) for dg in range(1, gy_count)], axis=0
    )
    column_values = values
    values = jnp.concatenate(
        [values] + [hop(values, 2 * p) for p in range(1, pairs)], axis=0
    )
    zero = zero_after(column_values[-1:])

    merged = jnp.concatenate([own, partner], axis=2)
    arriving = []
    for c in range(chunks):
        arriving.append([])
        for dg in range(gy_count):
            part = lax.dynamic_slice(
                merged,
                ((gy + dg + zero) % gy_count, c * chunk, 0, 0),
                (1, chunk, 2 * bands_local, planes),
            )[0]
            arriving[c].append(gy_shift(part, dg) if dg else part)

    grid = np.arange(planes, dtype=np.int64)
    table = np.cos((2.0 * np.pi / planes) * ((grid[:, None] * grid[None, :]) % planes))
    kernel = lax.dynamic_slice_in_dim(coulomb, me * half, half, 1).T
    lags = jnp.dot(
        kernel, jnp.asarray(table / planes, F32), precision=HIGH, preferred_element_type=F32
    )
    lags = jnp.stack([jnp.roll(lags, z * slab, axis=1) for z in (gz, gz ^ 1)])

    steps = n // 256
    gram = sweep_gram(values, None, 0, (lags,))

    fields = [None] * chunks
    rows = total_bands // pairs
    pending = None
    for step in range(1, steps):
        after = ()
        if step <= chunks:
            c = step - 1
            mine = wait_for(jnp.concatenate(arriving[c], axis=1), gram)
            after = (mine,)
            if pairs == 4:
                if pending is not None:
                    after = after + pending
                    fields[c - 1] = fields[c - 1] + relay(pending, gram)
                pending = (hop(mine, 2), hop(mine, 4))
                fields[c] = (mine,) + pending
            else:
                fields[c] = (mine,) + tuple(hop(mine, 2 * p) for p in range(1, pairs))
        elif pending is not None:
            after = pending
            fields[chunks - 1] = fields[chunks - 1] + relay(pending, gram)
            pending = None
        gram = sweep_gram(values, gram, step, after)
    inverse = gram

    weights = ()
    for c in range(chunks):
        after = (inverse,) if c else ()
        weights = convolve(fields[c], values, lags, slab, c * chunk, weights, after)
    own_weights, other_weights = weights
    other_weights = hop(other_weights, 1)
    blocks_of_16 = half // 16
    result = fit((me * blocks_of_16)[None], own_weights, inverse, col_block, ())
    return fit(((1 - me) * blocks_of_16)[None], other_weights, inverse, col_block, (result,))


def solution(mesh):
    return jax.shard_map(
        per_device,
        mesh=mesh,
        in_specs=(P(("gz", "gy"), None, None), P(), P(None, "gy")),
        out_specs=P("gz", "gy", None),
        check_vma=False,
    )
```
